512 devices in a mesh: region: 16 (over z, core), bulk: 32 (over y, x).
Axes of the slice: x: 4, y: 8, z: 8, core: 2. Of those that a mesh axis runs over, the one named last changes fastest.
Arguments:
- positions: float32 [32768, 3, 128], P(('region', 'bulk')), may hold values from -6 to 6
- fields: float32 [32768, 4, 128], P(('region', 'bulk')), may hold values from -6 to 6
- storage: float32 [32768, 128], P(('region', 'bulk')), may hold values from 0.5 to 2
- velocity: float32 [32768, 3, 128], P(('region', 'bulk')), may hold values from -4 to 4
- send_list: int32 [512, 3, 32, 1], P(('region', 'bulk')), may hold values from 0 to 63
- remote_local: int32 [512, 96, 2], P(('region', 'bulk')), may hold values from 0 to 63
- remote_mask: int32 [512, 96, 2, 16, 128], P(('region', 'bulk')), may hold values from 0 to 255
- local_pairs: int32 [512, 64, 2], P(('region', 'bulk')), may hold values from 0 to 63, as said below
- local_mask: int32 [512, 64, 16, 128], P(('region', 'bulk')), may hold values from 0 to 255
- migrate_list: int32 [512, 32, 1], P(('region', 'bulk')), may hold values from -1 to 63, as said below
Outputs:
- new_fields: float32 [32768, 4, 128], P(('region', 'bulk'))
- new_velocity: float32 [32768, 3, 128], P(('region', 'bulk'))
- arrived: float32 [16384, 11, 128], P(('region', 'bulk'))
The draws below stay inside these ranges and needn't reach their ends.
Inputs may be any that keep to these rules, and one draw needn't show every extreme that they name: `local_pairs`: each pair names two different owned blocks. `migrate_list`: owned blocks named on one device are distinct; in each region some devices hand 1 blocks to each of several peers and the rest hand none.
All inputs are finite; a program needn't handle non-finite values.
Results may differ from the reference program's by a relative error of at most 0.00002.
Values sent between devices are 32-bit elements; how exact they have to be, the bound alone decides.
No kernel may reach another device: no remote copies, remote signals or barrier semaphores. Data moves between devices by JAX's collectives and lax.ppermute only.
A program may use at most 64 MiB of HBM per device.

```python
import math
import jax
import jax.numpy as jnp
from jax import lax

PTS = 128
BLK_DEV = 64
SLOTS = 1
TOUCH = 2
MIG = 1
BLOCKS = 32768
RECV = 96
N_REGION = 16
N_BULK = 32


def mask_words(key, count):
    first_part = jax.random.randint(jax.random.fold_in(key, 1), (count, PTS // 8, PTS), 0, 256)
    second_part = jax.random.randint(jax.random.fold_in(key, 2), (count, PTS // 8, PTS), 0, 256)
    return jnp.bitwise_or(first_part, second_part).astype(jnp.int32)


def draw_remote_mask(key, part):
    key = jax.random.fold_in(key, 11)
    count = N_REGION * N_BULK * 3 * N_BULK * SLOTS * TOUCH
    return mask_words(key, count).reshape(N_REGION * N_BULK, 3 * N_BULK * SLOTS, TOUCH, PTS // 8, PTS)


def draw_local_mask(key, part):
    key = jax.random.fold_in(key, 17)
    count = N_REGION * N_BULK * BLK_DEV
    return mask_words(key, count).reshape(N_REGION * N_BULK, BLK_DEV, PTS // 8, PTS)


def draw_local_pairs(key, part):
    key = jax.random.fold_in(key, 23)
    first_block = jax.random.randint(jax.random.fold_in(key, 1), (N_REGION * N_BULK, BLK_DEV), 0, BLK_DEV)
    stride = jax.random.randint(jax.random.fold_in(key, 2), (N_REGION * N_BULK, BLK_DEV), 1, BLK_DEV)
    second_block = (first_block + stride) % BLK_DEV
    return jnp.stack([first_block, second_block], axis=-1).astype(jnp.int32)


def draw_migrate_list(key, part):
    key = jax.random.fold_in(key, 31)

    def one_device(device_key):
        return jax.random.permutation(device_key, BLK_DEV)[:N_BULK * MIG]

    def one_region(region_key):
        order = jax.random.permutation(jax.random.fold_in(region_key, 0), N_BULK)
        ranking = jnp.argsort(order)
        heavy = ranking < N_BULK // 2
        light = ranking >= N_BULK // 2
        device_keys = jax.random.split(jax.random.fold_in(region_key, 1), N_BULK)
        picks = jax.vmap(one_device)(device_keys).reshape(N_BULK, N_BULK, MIG)
        live = jnp.logical_and(heavy[:, None, None], light[None, :, None])
        return jnp.where(live, picks, -1)
    region_keys = jax.random.split(key, N_REGION)
    return jax.vmap(one_region)(region_keys).reshape(N_REGION * N_BULK, N_BULK, MIG).astype(jnp.int32)


def set_ends(result, own_key, smallest, largest):
    dims = result.shape
    place = [jax.random.randint(jax.random.fold_in(own_key, axis), (), 0, dims[axis]) for axis in range(len(dims))]
    result = result.at[tuple(place)].set(smallest)
    longest = dims.index(max(dims))
    place[longest] = (place[longest] + 1) % dims[longest]
    return result.at[tuple(place)].set(largest)


def steps_of(key, extent, cuts, low, top_value):
    level = 1.0
    for dim, shards_of in cuts:
        draws = jax.random.uniform(jax.random.fold_in(jax.random.fold_in(key, 6), dim), (shards_of,), jnp.float32, low / len(cuts), top_value / len(cuts))
        level = level * jnp.repeat(jnp.exp(draws), extent[dim] // shards_of).reshape((-1,) + (1,) * (len(extent) - 1 - dim))
    return level


def noise(rng, extent, scale, limit, cuts=(), kind=jnp.bfloat16):
    result = scale * jax.random.normal(rng, extent, jnp.float32)
    if cuts:
        result = result * steps_of(rng, extent, cuts, -0.22, 0.18)
    return jnp.clip(result, -limit, limit).astype(kind)


def setup_inputs(seed: int = 0) -> dict:
    key_list = jax.random.split(jax.random.key(seed), 11)
    return {
        "positions": noise(key_list[0], (BLOCKS, 3, PTS), 1.0, 6.0, ((0, 512),), jnp.float32),
        "fields": noise(key_list[1], (BLOCKS, 4, PTS), 1.0, 6.0, ((0, 512),), jnp.float32),
        "storage": jnp.clip(jnp.exp(math.log(2.0) - 1.3862944 * jax.random.uniform(key_list[2], (BLOCKS, PTS), jnp.float32) ** steps_of(key_list[2], (BLOCKS, PTS), ((0, 512),), -0.2, 0.2)), 0.5, 2.0),
        "velocity": noise(key_list[3], (BLOCKS, 3, PTS), 0.5, 4.0, ((0, 512),), jnp.float32),
        "send_list": set_ends(jax.random.randint(key_list[4], (N_REGION * N_BULK, 3, N_BULK, SLOTS), 0, BLK_DEV), jax.random.fold_in(key_list[4], 1), 0, BLK_DEV - 1).astype(jnp.int32),
        "remote_local": set_ends(jax.random.randint(key_list[5], (N_REGION * N_BULK, RECV, TOUCH), 0, BLK_DEV), jax.random.fold_in(key_list[5], 1), 0, BLK_DEV - 1).astype(jnp.int32),
        "remote_mask": draw_remote_mask(jax.random.fold_in(key_list[10], 71), 0),
        "local_pairs": draw_local_pairs(jax.random.fold_in(key_list[10], 71), 0),
        "local_mask": draw_local_mask(jax.random.fold_in(key_list[10], 71), 0),
        "migrate_list": draw_migrate_list(jax.random.fold_in(key_list[10], 71), 0),
    }


bond_stiff = 0.1
press_gain = 0.05
leak_gain = 0.5
time_step = 0.5
inv_horizon = 0.25
group_rows = 16


def unpack_bonds(packed):
    shifts = jnp.arange(8, dtype=jnp.int32)
    bit_table = jnp.bitwise_and(jnp.right_shift(packed[:, :, None, :], shifts[None, None, :, None]), 1)
    return bit_table.reshape(packed.shape[0], packed.shape[1] * 8, packed.shape[2]).astype(jnp.float32)


def tile_group(owned, others, packed):
    intact = unpack_bonds(packed)
    broken = 1.0 - intact
    apart = [others[:, k, :, None] - owned[:, k, None, :] for k in range(3)]
    dist_sq = apart[0] * apart[0] + apart[1] * apart[1] + apart[2] * apart[2]
    weight = 1.0 / (1.0 + inv_horizon * dist_sq)
    spring = bond_stiff * weight * intact
    leakage = weight * broken
    mean_press = 0.5 * (others[:, 6, :, None] + owned[:, 6, None, :])
    terms = [spring * (others[:, 3 + k, :, None] - owned[:, 3 + k, None, :]) - press_gain * leakage * mean_press * apart[k] for k in range(3)]
    terms.append(leak_gain * leakage * (others[:, 6, :, None] - owned[:, 6, None, :]))
    on_owned = jnp.stack([jnp.sum(t, axis=1) for t in terms], axis=1)
    on_others = jnp.stack([-jnp.sum(t, axis=2) for t in terms], axis=1)
    return on_owned, on_others


def tiles(owned, others, packed):
    count = owned.shape[0]
    groups = count // group_rows

    def one_group(items):
        return tile_group(items[0], items[1], items[2])

    on_owned, on_others = lax.map(one_group, (owned.reshape(groups, group_rows, 7, -1), others.reshape(groups, group_rows, 7, -1), packed.reshape(groups, group_rows, packed.shape[1], packed.shape[2])))
    return on_owned.reshape(count, 4, -1), on_others.reshape(count, 4, -1)


def device_terms(items):
    points, received, remote_local, remote_mask, local_pairs, local_mask = items
    slot_count, touch = remote_local.shape
    width = points.shape[2]
    flat_local = remote_local.reshape(-1)
    owned = points[flat_local]
    others = jnp.repeat(received, touch, axis=0)
    on_owned, on_others = tiles(owned, others, remote_mask.reshape(slot_count * touch, remote_mask.shape[2], remote_mask.shape[3]))
    totals = jnp.zeros((points.shape[0], 4, width), jnp.float32)
    totals = totals.at[flat_local].add(on_owned)
    slot_back = on_others.reshape(slot_count, touch, 4, width).sum(axis=1)
    first_block = local_pairs[:, 0]
    second_block = local_pairs[:, 1]
    pair_first, pair_second = tiles(points[first_block], points[second_block], local_mask)
    totals = totals.at[first_block].add(pair_first).at[second_block].add(pair_second)
    return totals, slot_back


def take_rows(source, picks):
    return source[picks]


def add_rows(totals, picks, terms):
    return totals.at[picks].add(terms)


def reference(positions, fields, storage, velocity, send_list, remote_local, remote_mask, local_pairs, local_mask, migrate_list):
    nreg = N_REGION
    nbulk = N_BULK
    points = jnp.concatenate([positions, fields], axis=1).reshape(nreg, nbulk, BLK_DEV, 7, PTS)
    sends = send_list.reshape(nreg, nbulk, 3, nbulk, SLOTS)
    pieces = []
    for direction in range(3):
        offset = direction - 1
        rolled_pts = jnp.roll(points, offset, axis=0)
        rolled_idx = jnp.roll(sends[:, :, direction], offset, axis=0).reshape(nreg, nbulk, nbulk * SLOTS)
        picked = jax.vmap(jax.vmap(take_rows))(rolled_pts, rolled_idx)
        picked = picked.reshape(nreg, nbulk, nbulk, SLOTS, 7, PTS).transpose(0, 2, 1, 3, 4, 5)
        pieces.append(picked)
    received = jnp.stack(pieces, axis=2).reshape(nreg * nbulk, 3 * nbulk * SLOTS, 7, PTS)
    totals, slot_back = lax.map(device_terms, (points.reshape(nreg * nbulk, BLK_DEV, 7, PTS), received, remote_local, remote_mask, local_pairs, local_mask))
    back = slot_back.reshape(nreg, nbulk, 3, nbulk, SLOTS, 4, PTS)
    totals = totals.reshape(nreg, nbulk, BLK_DEV, 4, PTS)
    for direction in range(3):
        offset = direction - 1
        piece = back[:, :, direction].transpose(0, 2, 1, 3, 4, 5)
        piece = jnp.roll(piece, -offset, axis=0).reshape(nreg, nbulk, nbulk * SLOTS, 4, PTS)
        picks = sends[:, :, direction].reshape(nreg, nbulk, nbulk * SLOTS)
        totals = jax.vmap(jax.vmap(add_rows))(totals, picks, piece)
    totals = totals.reshape(-1, 4, PTS)
    new_velocity = velocity + time_step * totals[:, :3]
    displace = fields[:, :3] + time_step * new_velocity
    pressure = fields[:, 3] + time_step * totals[:, 3] / storage
    new_fields = jnp.concatenate([displace, pressure[:, None, :]], axis=1)
    moving = jnp.concatenate([new_fields, new_velocity, positions, storage[:, None, :]], axis=1).reshape(nreg, nbulk, BLK_DEV, 11, PTS)
    moves = migrate_list.reshape(nreg, nbulk, nbulk * MIG)
    chosen = jax.vmap(jax.vmap(take_rows))(moving, jnp.maximum(moves, 0))
    chosen = jnp.where((moves >= 0)[..., None, None], chosen, 0.0)
    arrived = chosen.reshape(nreg, nbulk, nbulk, MIG, 11, PTS).transpose(0, 2, 1, 3, 4, 5).reshape(-1, 11, PTS)
    return new_fields, new_velocity, arrived
```

```python
import functools

import jax
import jax.numpy as jnp
from jax import lax
from jax.experimental import pallas as pl
from jax.experimental.pallas import tpu as pltpu
from jax.sharding import PartitionSpec as P

bond_stiff = 0.1
press_gain = 0.05
leak_gain = 0.5
time_step = 0.5
inv_horizon = 0.25
vmem_bytes = 40 * 1024 * 1024
f32 = jnp.float32
bf16 = jnp.bfloat16


def from_behind(shard, axis, by):
    peers = lax.axis_size(axis)
    return lax.ppermute(shard, axis, [(i, (i + by) % peers) for i in range(peers)])


def features(block):
    width = block.shape[1]
    x, p, u = block[0:3], block[3:4], block[4:7]
    one = jnp.ones((1, width), f32)
    rows = jnp.concatenate([x, p, p * x, one, u, one, jnp.zeros((4, width), f32)], axis=0)
    high = rows.astype(bf16)
    rest = rows - high.astype(f32)
    middle = rest.astype(bf16)
    low = (rest - middle.astype(f32)).astype(bf16)
    return jnp.concatenate([high, middle, low], axis=0)


def terms_of(sums, x, p, u):
    mean_gain = 0.5 * press_gain
    out = [
        bond_stiff * (sums[8 + k] - u[k] * sums[11])
        - mean_gain * (p * (sums[k] - x[k] * sums[7]) + (sums[4 + k] - x[k] * sums[3]))
        for k in range(3)
    ]
    out.append(leak_gain * (sums[3] - p * sums[7]))
    return out


def block_rows(ref, first, count, stride):
    return ref[pl.ds(first, count, stride=stride), :]


def columns(blocks_ref, turned_ref):
    for g in range(turned_ref.shape[0]):
        turned_ref[g] = jnp.transpose(blocks_ref[pl.ds(g * 128, 128), :])


def bond_weights(others, owned, words, bits):
    apart = [others[k] - 0.5 * owned[k : k + 1] for k in range(3)]
    size = apart[0] * apart[0] + 1.0 + (apart[1] * apart[1] + apart[2] * apart[2])
    weight = pltpu.reciprocal(size, approx=True)
    intact = (words & bits) != 0
    high = weight.astype(bf16)
    high_wide = high.astype(f32)
    low_wide = weight - high_wide
    low = low_wide.astype(bf16)
    intact_high = jnp.where(intact, high_wide, 0.0).astype(bf16)
    intact_low = jnp.where(intact, low_wide, 0.0).astype(bf16)
    return intact_high, high, intact_low, low


def split_sums(product):
    product = product[0:16] + product[16:32] + product[32:48]
    intact, every = product[:, :128], product[:, 128:]
    return jnp.concatenate([every[0:8] - intact[0:8], intact[8:16]], axis=0)


def tile_sums(weights, owned_feature, other_feature):
    intact_high, high, intact_low, low = weights
    by_other = jnp.concatenate(
        [
            jnp.concatenate([intact_high, high], axis=1),
            jnp.concatenate([intact_low, low], axis=1),
        ],
        axis=0,
    )
    on_owned = jnp.dot(
        jnp.concatenate([other_feature, other_feature], axis=1),
        by_other,
        preferred_element_type=f32,
    )
    by_owned = jnp.concatenate(
        [
            jnp.concatenate([intact_high, intact_low], axis=1),
            jnp.concatenate([high, low], axis=1),
        ],
        axis=0,
    )
    on_other = lax.dot_general(
        jnp.concatenate([owned_feature, owned_feature], axis=1),
        by_owned,
        (((1,), (1,)), ((), ())),
        preferred_element_type=f32,
    )
    return split_sums(on_owned), split_sums(on_other)


def tile_loop(
    slots, touch, per_step, owned_of, mask_ref, other_blocks, other_feature, turned_ref, points_ref,
    feature_ref, sums_ref, weights_ref, other_of, store_other,
):
    bits = jnp.left_shift(1, lax.broadcasted_iota(jnp.int32, (16, 8, 128), 1)).reshape(128, 128)
    steps = slots // per_step

    def weigh(step, half):
        for n in range(per_step):
            slot = step * per_step + n
            other = other_of(slot)
            turned = pltpu.roll(turned_ref[other // 16], lax.rem(128 - 8 * lax.rem(other, 16), 128), 1)
            others = [jnp.broadcast_to(0.5 * turned[:, k : k + 1], (128, 128)) for k in range(3)]
            for e in range(touch):
                tile = slot * touch + e
                owned = owned_of(slot, e)
                words = jnp.broadcast_to(mask_ref[tile][:, None, :], (16, 8, 128)).reshape(128, 128)
                a, b, c, d = bond_weights(others, points_ref[owned], words, bits)
                at = n * touch + e
                weights_ref[half, at, 0:128, 0:128] = a
                weights_ref[half, at, 0:128, 128:256] = b
                weights_ref[half, at, 128:256, 0:128] = c
                weights_ref[half, at, 128:256, 128:256] = d

    def add_up(step, half):
        for n in range(per_step):
            slot = step * per_step + n
            feature = other_feature(slot)
            on_other = None
            for e in range(touch):
                owned = owned_of(slot, e)
                kept = weights_ref[half, n * touch + e]
                parts = (kept[:128, :128], kept[:128, 128:], kept[128:, :128], kept[128:, 128:])
                on_owned, more = tile_sums(parts, feature_ref[owned], feature)
                sums_ref[owned] += on_owned
                on_other = more if on_other is None else on_other + more
            store_other(slot, on_other)

    weigh(0, 0)

    def body(k, carry):
        weigh(2 * k + 1, 1)
        add_up(2 * k, 0)
        weigh(jnp.minimum(2 * k + 2, steps - 1), 0)
        add_up(2 * k + 1, 1)
        return carry

    lax.fori_loop(0, steps // 2, body, 0)


def owned_terms(sums_ref, points_ref, count):
    rows = sums_ref.reshape(count * 16, 128)
    sums = [block_rows(rows, r, count, 16) for r in range(12)]
    flat = points_ref.reshape(count * 8, 128)
    own = [block_rows(flat, r, count, 8) for r in range(7)]
    return terms_of(sums, own[0:3], own[3], own[4:7])


def pack_kernel(sends_ref, moves_ref, positions_ref, fields_ref, out_ref, points_ref):
    count = positions_ref.shape[1]
    peers = out_ref.shape[0]
    flat = points_ref.reshape(count * 8, 128)
    for k in range(3):
        flat[pl.ds(k, count, stride=8), :] = positions_ref[k]
        flat[pl.ds(4 + k, count, stride=8), :] = block_rows(fields_ref, k, count, 4)
    flat[pl.ds(3, count, stride=8), :] = block_rows(fields_ref, 3, count, 4)
    flat[pl.ds(7, count, stride=8), :] = jnp.zeros((count, 128), f32)

    def one_peer(peer, carry):
        move = moves_ref[0, 0, peer]
        live = (move >= 0).astype(f32)
        moved = points_ref[jnp.maximum(move, 0)] * live
        for o in range(3):
            out_ref[peer, 8 * o : 8 * o + 7] = points_ref[sends_ref[o, 0, peer], 0:7]
            out_ref[peer, 8 * o + 7 : 8 * o + 8] = moved[o : o + 1]
        return carry

    lax.fori_loop(0, peers, one_peer, 0, unroll=8)


def local_kernel(pairs_ref, points_ref, mask_ref, totals_ref, feature_ref, sums_ref, turned_ref, weights_ref):
    count = points_ref.shape[0]
    tiles = mask_ref.shape[0]
    sums_ref[...] = jnp.zeros_like(sums_ref)
    columns(points_ref.reshape(count * 8, 128), turned_ref)

    def one_block(block, carry):
        feature_ref[block] = features(points_ref[block])
        return carry

    lax.fori_loop(0, count, one_block, 0, unroll=4)

    def store_other(slot, on_other):
        sums_ref[pairs_ref[1, slot]] += on_other

    tile_loop(
        tiles, 1, 4, lambda slot, e: pairs_ref[0, slot], mask_ref, None,
        lambda slot: feature_ref[pairs_ref[1, slot]], turned_ref, points_ref, feature_ref, sums_ref,
        weights_ref, lambda slot: pairs_ref[1, slot], store_other,
    )
    for k, row in enumerate(owned_terms(sums_ref, points_ref, count)):
        totals_ref[k] = row


def remote_kernel(
    groups, local_ref, totals_in_ref, points_ref, feature_ref, *rest
):
    lifted = rest[: len(groups)]
    masks = rest[len(groups) : 2 * len(groups)]
    totals_ref = rest[2 * len(groups)]
    back = rest[2 * len(groups) + 1 : 3 * len(groups) + 1]
    sums_ref, turned_ref, weights_ref, other_sums = rest[3 * len(groups) + 1 :]
    count = points_ref.shape[0]
    slots = lifted[0].shape[0]
    sums_ref[...] = jnp.zeros_like(sums_ref)
    for part, group in enumerate(groups):
        blocks = lifted[part]
        columns(blocks.reshape(slots * 8, 128), turned_ref)

        def store_other(slot, on_other):
            other_sums[slot] = on_other

        tile_loop(
            slots, 2, 2, lambda slot, e: local_ref[e, group * slots + slot], masks[part], None,
            lambda slot: features(blocks[slot]), turned_ref, points_ref, feature_ref, sums_ref,
            weights_ref, lambda slot: slot, store_other,
        )
        back_rows = back[part].reshape(slots * 4, 128)
        for k, row in enumerate(owned_terms(other_sums, blocks, slots)):
            back_rows[pl.ds(k, slots, stride=4), :] = row
    for k, row in enumerate(owned_terms(sums_ref, points_ref, count)):
        totals_ref[k] = totals_in_ref[k] + row


def update_kernel(
    sends_ref, moves_ref, totals_ref, returned_ref, fields_ref, velocity_ref, storage_ref,
    new_fields_ref, new_velocity_ref, moving_ref, sums_ref, rows_ref,
):
    count = storage_ref.shape[0]
    peers = returned_ref.shape[0]
    sums_ref[...] = jnp.zeros_like(sums_ref)

    def one_peer(peer, carry):
        for o in range(3):
            sums_ref[sends_ref[o, 0, peer]] += returned_ref[peer, 4 * o : 4 * o + 4]
        return carry

    lax.fori_loop(0, peers, one_peer, 0, unroll=4)
    sums = sums_ref.reshape(count * 4, 128)
    rows = rows_ref.reshape(count * 8, 128)
    for k in range(3):
        speed = velocity_ref[k] + time_step * (totals_ref[k] + block_rows(sums, k, count, 4))
        moved = block_rows(fields_ref, k, count, 4) + time_step * speed
        new_velocity_ref[k] = speed
        new_fields_ref[pl.ds(k, count, stride=4), :] = moved
        rows[pl.ds(k, count, stride=8), :] = moved
        rows[pl.ds(4 + k, count, stride=8), :] = speed
    stored = storage_ref[...]
    pressure = (
        block_rows(fields_ref, 3, count, 4)
        + time_step * (totals_ref[3] + block_rows(sums, 3, count, 4)) / stored
    )
    new_fields_ref[pl.ds(3, count, stride=4), :] = pressure
    rows[pl.ds(3, count, stride=8), :] = pressure
    rows[pl.ds(7, count, stride=8), :] = stored

    def one_move(peer, carry):
        move = moves_ref[0, 0, peer]
        moving_ref[peer] = rows_ref[jnp.maximum(move, 0)] * (move >= 0).astype(f32)
        return carry

    lax.fori_loop(0, peers, one_move, 0, unroll=4)


def arrive_kernel(late_ref, early_ref, out_ref):
    peers = late_ref.shape[0]
    late = late_ref.reshape(peers * 8, 128)
    early = early_ref.reshape(peers * 24, 128)
    for k in range(7):
        out_ref[k] = block_rows(late, k, peers, 8)
    for k in range(3):
        out_ref[7 + k] = block_rows(early, 8 * k + 7, peers, 24)
    out_ref[10] = block_rows(late, 7, peers, 8)


def in_vmem():
    return pl.BlockSpec(memory_space=pltpu.VMEM)


def in_smem():
    return pl.BlockSpec(memory_space=pltpu.SMEM)


def params():
    return pltpu.CompilerParams(vmem_limit_bytes=vmem_bytes)


def cost(flops):
    return pl.CostEstimate(flops=flops, bytes_accessed=2 * 1024 * 1024, transcendentals=0)


def shape(*dims, dtype=f32):
    return jax.ShapeDtypeStruct(dims, dtype)


def remote_tiles(groups, local, totals, points, feature, lifted, mask):
    count = points.shape[0]
    slots = lifted[0].shape[0]
    tiles = 2 * slots
    return pl.pallas_call(
        functools.partial(remote_kernel, groups),
        grid=(1,),
        out_shape=[shape(4, count, 128)] + [shape(slots, 4, 128)] * len(groups),
        in_specs=[in_smem()]
        + [in_vmem()] * (3 + len(groups))
        + [pl.BlockSpec((tiles, 16, 128), functools.partial(lambda g, i: (g, 0, 0), g)) for g in groups],
        out_specs=[in_vmem()] * (1 + len(groups)),
        scratch_shapes=[
            pltpu.VMEM((count, 16, 128), f32),
            pltpu.VMEM((slots // 16, 128, 128), f32),
            pltpu.VMEM((2, 4, 256, 256), bf16),
            pltpu.VMEM((slots, 16, 128), f32),
        ],
        compiler_params=params(),
        cost_estimate=cost(len(groups) * 4 * 10**9),
        name="remote_tiles",
    )(local, totals, points, feature, *lifted, *([mask] * len(groups)))


def per_device(
    positions,
    fields,
    storage,
    velocity,
    send_list,
    remote_local,
    remote_mask,
    local_pairs,
    local_mask,
    migrate_list,
):
    count = positions.shape[0]
    peers = send_list.shape[2]
    sends = send_list[0].transpose(0, 2, 1)
    moves = migrate_list.transpose(0, 2, 1)
    rows_first = positions.transpose(1, 0, 2)
    flat_fields = fields.reshape(count * 4, 128)
    outgoing, points = pl.pallas_call(
        pack_kernel,
        out_shape=[shape(peers, 24, 128), shape(count, 8, 128)],
        in_specs=[in_smem(), in_smem(), in_vmem(), in_vmem()],
        out_specs=[in_vmem()] * 2,
        compiler_params=params(),
        name="pack",
    )(sends, moves, rows_first, flat_fields)
    spread = lax.all_to_all(outgoing, "bulk", split_axis=0, concat_axis=0, tiled=True)
    pairs = local_pairs[0].transpose(1, 0)
    tiles = local_mask.shape[1]
    totals, feature = pl.pallas_call(
        local_kernel,
        out_shape=[shape(4, count, 128), shape(count, 48, 128, dtype=bf16)],
        in_specs=[in_smem(), in_vmem(), in_vmem()],
        out_specs=[in_vmem()] * 2,
        scratch_shapes=[
            pltpu.VMEM((count, 16, 128), f32),
            pltpu.VMEM((count // 16, 128, 128), f32),
            pltpu.VMEM((2, 4, 256, 256), bf16),
        ],
        compiler_params=params(),
        cost_estimate=cost(4 * 10**9),
        name="local_tiles",
    )(pairs, points, local_mask[0])
    lifted = [
        from_behind(spread[:, 8 * (offset + 1) : 8 * (offset + 1) + 8], "region", offset)
        for offset in (-1, 1)
    ]
    local = remote_local[0].transpose(1, 0)
    mask = remote_mask[0].reshape(-1, remote_mask.shape[3], remote_mask.shape[4])
    totals, here_back = remote_tiles((1,), local, totals, points, feature, [spread[:, 8:16]], mask)
    totals, down_back, up_back = remote_tiles((0, 2), local, totals, points, feature, lifted, mask)
    lowered = [from_behind(part, "region", -offset) for part, offset in ((down_back, -1), (up_back, 1))]
    stacked = jnp.concatenate([lowered[0], here_back, lowered[1]], axis=1)
    returned = lax.all_to_all(stacked, "bulk", split_axis=0, concat_axis=0, tiled=True)
    new_fields, new_velocity, moving = pl.pallas_call(
        update_kernel,
        out_shape=[shape(count * 4, 128), shape(3, count, 128), shape(peers, 8, 128)],
        in_specs=[in_smem()] * 2 + [in_vmem()] * 5,
        out_specs=[in_vmem()] * 3,
        scratch_shapes=[pltpu.VMEM((count, 4, 128), f32), pltpu.VMEM((count, 8, 128), f32)],
        compiler_params=params(),
        name="update",
    )(sends, moves, totals, returned, flat_fields, velocity.transpose(1, 0, 2), storage)
    late = lax.all_to_all(moving, "bulk", split_axis=0, concat_axis=0, tiled=True)
    arrived = pl.pallas_call(
        arrive_kernel,
        out_shape=shape(11, peers, 128),
        in_specs=[in_vmem()] * 2,
        out_specs=in_vmem(),
        compiler_params=params(),
        name="arrive",
    )(late, spread)
    return (
        new_fields.reshape(count, 4, 128),
        new_velocity.transpose(1, 0, 2),
        arrived.transpose(1, 0, 2),
    )


def solution(mesh):
    spec = lambda rank: P(("region", "bulk"), *([None] * (rank - 1)))
    return jax.shard_map(
        per_device,
        mesh=mesh,
        in_specs=tuple(spec(rank) for rank in (3, 3, 2, 3, 4, 3, 5, 3, 4, 3)),
        out_specs=(spec(3), spec(3), spec(3)),
        check_vma=False,
    )
```

```python
import functools

import jax
import jax.numpy as jnp
from jax import lax
from jax.experimental import pallas as pl
from jax.experimental.pallas import tpu as pltpu
from jax.sharding import PartitionSpec as P

bond_stiff = 0.1
press_gain = 0.05
leak_gain = 0.5
time_step = 0.5
inv_horizon = 0.25
vmem_bytes = 40 * 1024 * 1024
f32 = jnp.float32
bf16 = jnp.bfloat16


def from_behind(shard, axis, by):
    peers = lax.axis_size(axis)
    return lax.ppermute(shard, axis, [(i, (i + by) % peers) for i in range(peers)])


def features(block):
    width = block.shape[1]
    x, p, u = block[0:3], block[3:4], block[4:7]
    one = jnp.ones((1, width), f32)
    rows = jnp.concatenate([x, p, p * x, one, u, one, jnp.zeros((4, width), f32)], axis=0)
    high = rows.astype(bf16)
    rest = rows - high.astype(f32)
    middle = rest.astype(bf16)
    low = (rest - middle.astype(f32)).astype(bf16)
    return jnp.concatenate([high, middle, low], axis=0)


def terms_of(sums, x, p, u):
    mean_gain = 0.5 * press_gain
    out = [
        bond_stiff * (sums[8 + k] - u[k] * sums[11])
        - mean_gain * (p * (sums[k] - x[k] * sums[7]) + (sums[4 + k] - x[k] * sums[3]))
        for k in range(3)
    ]
    out.append(leak_gain * (sums[3] - p * sums[7]))
    return out


def block_rows(ref, first, count, stride):
    return ref[pl.ds(first, count, stride=stride), :]


def turn(blocks, turned_ref):
    for g in range(turned_ref.shape[0]):
        group = jnp.concatenate([blocks(16 * g + n) for n in range(16)], axis=0)
        turned_ref[g] = 0.5 * jnp.transpose(group)


def bond_weights(others, owned, words, bits):
    apart = [others[k] - 0.5 * owned[k : k + 1] for k in range(3)]
    size = apart[0] * apart[0] + 1.0 + (apart[1] * apart[1] + apart[2] * apart[2])
    weight = pltpu.reciprocal(size, approx=True)
    intact = (words & bits) != 0
    high = weight.astype(bf16)
    low = (weight - high.astype(f32)).astype(bf16)
    none = jnp.zeros((128, 128), bf16)
    intact_high = jnp.where(intact, high, none)
    intact_low = jnp.where(intact, low, none)
    return intact_high, high, intact_low, low


def split_sums(product):
    product = product[0:16] + product[16:32] + product[32:48]
    intact, every = product[:, :128], product[:, 128:]
    return jnp.concatenate([every[0:8] - intact[0:8], intact[8:16]], axis=0)


def tile_sums(weights, owned_feature, other_feature):
    intact_high, high, intact_low, low = weights
    by_other = jnp.concatenate(
        [
            jnp.concatenate([intact_high, high], axis=1),
            jnp.concatenate([intact_low, low], axis=1),
        ],
        axis=0,
    )
    on_owned = jnp.dot(
        jnp.concatenate([other_feature, other_feature], axis=1),
        by_other,
        preferred_element_type=f32,
    )
    by_owned = jnp.concatenate(
        [
            jnp.concatenate([intact_high, intact_low], axis=1),
            jnp.concatenate([high, low], axis=1),
        ],
        axis=0,
    )
    on_other = lax.dot_general(
        jnp.concatenate([owned_feature, owned_feature], axis=1),
        by_owned,
        (((1,), (1,)), ((), ())),
        preferred_element_type=f32,
    )
    return split_sums(on_owned), split_sums(on_other)


def tile_loop(
    slots, touch, per_step, owned_of, other_of, other_block, mask_ref, turned_ref, points_ref,
    feature_ref, sums_ref, weights_ref, other_feature_ref, store_other,
):
    bits = jnp.left_shift(1, lax.broadcasted_iota(jnp.int32, (16, 8, 128), 1)).reshape(128, 128)
    steps = slots // per_step

    def weigh(step, half):
        for n in range(per_step):
            slot = step * per_step + n
            other = other_of(slot)
            if other_block is not None:
                other_feature_ref[half, n] = features(other_block(slot))
            turned = turned_ref[other // 16]
            lane = 8 * lax.rem(other, 16)
            others = [
                jnp.take_along_axis(turned, jnp.full((128, 128), lane + k, jnp.int32), axis=1)
                for k in range(3)
            ]
            for e in range(touch):
                tile = slot * touch + e
                owned = owned_of(slot, e)
                words = jnp.concatenate(
                    [mask_ref[tile, pl.ds(j, 8, stride=0), :] for j in range(16)], axis=0
                )
                a, b, c, d = bond_weights(others, points_ref[owned], words, bits)
                at = n * touch + e
                weights_ref[half, at, 0:128, 0:128] = a
                weights_ref[half, at, 0:128, 128:256] = b
                weights_ref[half, at, 128:256, 0:128] = c
                weights_ref[half, at, 128:256, 128:256] = d

    def add_up(step, half):
        for n in range(per_step):
            slot = step * per_step + n
            if other_block is not None:
                feature = other_feature_ref[half, n]
            else:
                feature = feature_ref[other_of(slot)]
            on_other = None
            for e in range(touch):
                owned = owned_of(slot, e)
                kept = weights_ref[half, n * touch + e]
                parts = (kept[:128, :128], kept[:128, 128:], kept[128:, :128], kept[128:, 128:])
                on_owned, more = tile_sums(parts, feature_ref[owned], feature)
                sums_ref[owned] += on_owned
                on_other = more if on_other is None else on_other + more
            store_other(slot, on_other)

    weigh(0, 0)

    def body(k, carry):
        weigh(2 * k + 1, 1)
        add_up(2 * k, 0)
        weigh(2 * k + 2, 0)
        add_up(2 * k + 1, 1)
        return carry

    lax.fori_loop(0, steps // 2 - 1, body, 0)
    weigh(steps - 1, 1)
    add_up(steps - 2, 0)
    add_up(steps - 1, 1)


def owned_terms(sums_ref, points, count):
    rows = sums_ref.reshape(sums_ref.shape[0] * 16, 128)
    return lambda first: terms_of(
        [block_rows(rows, first * 16 + r, count, 16) for r in range(12)],
        [points(r) for r in range(3)],
        points(3),
        [points(4 + r) for r in range(3)],
    )


def fetch(copies):
    for copy in copies:
        copy.start()
    for copy in copies:
        copy.wait()


def pack_kernel(
    sends_any, moves_any, positions_any, fields_any, down_ref, here_ref, up_ref, going_ref, points_ref,
    sends_ref, moves_ref, positions_ref, fields_ref, sems,
):
    pairs = (
        (positions_any, positions_ref),
        (fields_any, fields_ref),
        (sends_any, sends_ref),
        (moves_any, moves_ref),
    )
    fetch([pltpu.make_async_copy(a, b, sems.at[n]) for n, (a, b) in enumerate(pairs)])
    count = positions_ref.shape[1]
    peers = here_ref.shape[0]
    flat = points_ref.reshape(count * 8, 128)
    for k in range(3):
        flat[pl.ds(k, count, stride=8), :] = positions_ref[k]
        flat[pl.ds(4 + k, count, stride=8), :] = block_rows(fields_ref, k, count, 4)
    flat[pl.ds(3, count, stride=8), :] = block_rows(fields_ref, 3, count, 4)
    flat[pl.ds(7, count, stride=8), :] = jnp.zeros((count, 128), f32)

    def one_peer(peer, carry):
        for o, out in enumerate((down_ref, here_ref, up_ref)):
            out[peer] = points_ref[sends_ref[o, 0, peer]]
        move = moves_ref[0, 0, peer]
        block = points_ref[jnp.maximum(move, 0)]
        going_ref[peer] = jnp.where(move >= 0, block, jnp.zeros_like(block))
        return carry

    lax.fori_loop(0, peers, one_peer, 0, unroll=8)


def merge_kernel(going_ref, down_ref, here_ref, up_ref, out_ref):
    last = lax.broadcasted_iota(jnp.int32, (8, 128), 0) == 7

    def one_peer(peer, carry):
        block = going_ref[peer]
        for o, part in enumerate((down_ref, here_ref, up_ref)):
            out_ref[peer, 8 * o : 8 * o + 8] = jnp.where(last, block[o : o + 1], part[peer])
        return carry

    lax.fori_loop(0, out_ref.shape[0], one_peer, 0, unroll=8)


def local_kernel(
    pairs_ref, points_ref, mask_ref, totals_ref, feature_ref, sums_ref, turned_ref, weights_ref
):
    count = points_ref.shape[0]
    tiles = mask_ref.shape[0]
    sums_ref[...] = jnp.zeros_like(sums_ref)
    turn(lambda n: points_ref[n], turned_ref)

    def one_block(block, carry):
        feature_ref[block] = features(points_ref[block])
        return carry

    lax.fori_loop(0, count, one_block, 0, unroll=8)

    def store_other(slot, on_other):
        sums_ref[pairs_ref[1, slot]] += on_other

    tile_loop(
        tiles, 1, 4, lambda slot, e: pairs_ref[0, slot], lambda slot: pairs_ref[1, slot], None,
        mask_ref, turned_ref, points_ref, feature_ref, sums_ref, weights_ref, None, store_other,
    )
    flat = points_ref.reshape(count * 8, 128)
    terms = owned_terms(sums_ref, lambda r: block_rows(flat, r, count, 8), count)
    for k, row in enumerate(terms(0)):
        totals_ref[k] = row


def remote_kernel(groups, local_ref, totals_in_ref, points_ref, feature_ref, spread_ref, mask_any, *rest):
    totals_ref = rest[0]
    back = rest[1 : 1 + len(groups)]
    (sums_ref, turned_ref, weights_ref, other_feature_ref, other_sums, mask_ref, sems) = rest[
        1 + len(groups) :
    ]
    count = points_ref.shape[0]
    peers = spread_ref.shape[0]
    slots = peers * len(groups)
    tiles = 2 * peers
    copies = [
        pltpu.make_async_copy(
            mask_any.at[pl.ds(group * tiles, tiles)], mask_ref.at[pl.ds(part * tiles, tiles)], sems.at[part]
        )
        for part, group in enumerate(groups)
    ]
    for copy in copies:
        copy.start()
    first = groups[0]
    apart = groups[-1] - first

    def group_of(slot):
        return first + apart * (slot // peers), lax.rem(slot, peers)

    def other_block(slot):
        group, peer = group_of(slot)
        return spread_ref[peer, pl.ds(pl.multiple_of(8 * group, 8), 8)]

    def owned_of(slot, e):
        group, peer = group_of(slot)
        return local_ref[e, group * peers + peer]

    sums_ref[...] = jnp.zeros_like(sums_ref)
    turn(
        lambda n: spread_ref[n % peers, 8 * groups[n // peers] : 8 * groups[n // peers] + 8], turned_ref
    )
    for copy in copies:
        copy.wait()

    def store_other(slot, on_other):
        other_sums[slot] = on_other

    tile_loop(
        slots, 2, 2, owned_of, lambda slot: slot, other_block, mask_ref, turned_ref, points_ref,
        feature_ref, sums_ref, weights_ref, other_feature_ref, store_other,
    )
    flat = spread_ref.reshape(peers * 24, 128)
    for part, group in enumerate(groups):
        terms = owned_terms(other_sums, lambda r: block_rows(flat, 8 * group + r, peers, 24), peers)
        back_rows = back[part].reshape(peers * 4, 128)
        for k, row in enumerate(terms(part * peers)):
            back_rows[pl.ds(k, peers, stride=4), :] = row
    own = points_ref.reshape(count * 8, 128)
    terms = owned_terms(sums_ref, lambda r: block_rows(own, r, count, 8), count)
    for k, row in enumerate(terms(0)):
        totals_ref[k] = totals_in_ref[k] + row


def update_kernel(
    sends_ref, moves_ref, totals_ref, returned_ref, fields_ref, velocity_ref, storage_ref,
    new_fields_ref, new_velocity_ref, moving_ref, sums_ref, rows_ref,
):
    count = storage_ref.shape[0]
    peers = returned_ref.shape[0]
    sums_ref[...] = jnp.zeros_like(sums_ref)

    def one_peer(peer, carry):
        for o in range(3):
            sums_ref[sends_ref[o, 0, peer]] += returned_ref[peer, o]
        return carry

    lax.fori_loop(0, peers, one_peer, 0, unroll=4)
    sums = sums_ref.reshape(count * 4, 128)
    rows = rows_ref.reshape(count * 8, 128)
    for k in range(3):
        speed = velocity_ref[k] + time_step * (totals_ref[k] + block_rows(sums, k, count, 4))
        moved = block_rows(fields_ref, k, count, 4) + time_step * speed
        new_velocity_ref[k] = speed
        new_fields_ref[pl.ds(k, count, stride=4), :] = moved
        rows[pl.ds(k, count, stride=8), :] = moved
        rows[pl.ds(4 + k, count, stride=8), :] = speed
    stored = storage_ref[...]
    pressure = (
        block_rows(fields_ref, 3, count, 4)
        + time_step * (totals_ref[3] + block_rows(sums, 3, count, 4)) / stored
    )
    new_fields_ref[pl.ds(3, count, stride=4), :] = pressure
    rows[pl.ds(3, count, stride=8), :] = pressure
    rows[pl.ds(7, count, stride=8), :] = stored

    def one_move(peer, carry):
        move = moves_ref[0, 0, peer]
        block = rows_ref[jnp.maximum(move, 0)]
        moving_ref[peer] = jnp.where(move >= 0, block, jnp.zeros_like(block))
        return carry

    lax.fori_loop(0, peers, one_move, 0, unroll=4)


def arrive_kernel(late_ref, early_ref, out_ref):
    peers = late_ref.shape[0]
    late = late_ref.reshape(peers * 8, 128)
    early = early_ref.reshape(peers * 24, 128)
    for k in range(7):
        out_ref[k] = block_rows(late, k, peers, 8)
    for k in range(3):
        out_ref[7 + k] = block_rows(early, 8 * k + 7, peers, 24)
    out_ref[10] = block_rows(late, 7, peers, 8)


def in_vmem():
    return pl.BlockSpec(memory_space=pltpu.VMEM)


def in_smem():
    return pl.BlockSpec(memory_space=pltpu.SMEM)


def params():
    return pltpu.CompilerParams(vmem_limit_bytes=vmem_bytes)


def cost(flops):
    return pl.CostEstimate(flops=flops, bytes_accessed=2 * 1024 * 1024, transcendentals=0)


def shape(*dims, dtype=f32):
    return jax.ShapeDtypeStruct(dims, dtype)


def anywhere():
    return pl.BlockSpec(memory_space=pl.ANY)


def remote_tiles(groups, local, totals, points, feature, spread, mask):
    count = points.shape[0]
    peers = spread.shape[0]
    slots = peers * len(groups)
    return pl.pallas_call(
        functools.partial(remote_kernel, groups),
        out_shape=[shape(4, count, 128)] + [shape(peers, 4, 128)] * len(groups),
        in_specs=[in_smem()] + [in_vmem()] * 4 + [anywhere()],
        out_specs=[in_vmem()] * (1 + len(groups)),
        scratch_shapes=[
            pltpu.VMEM((count, 16, 128), f32),
            pltpu.VMEM((slots // 16, 128, 128), f32),
            pltpu.VMEM((2, 4, 256, 256), bf16),
            pltpu.VMEM((2, 2, 48, 128), bf16),
            pltpu.VMEM((slots, 16, 128), f32),
            pltpu.VMEM((2 * slots, 16, 128), jnp.int32),
            pltpu.SemaphoreType.DMA((len(groups),)),
        ],
        compiler_params=params(),
        cost_estimate=cost(len(groups) * 4 * 10**9),
        name="remote_tiles",
    )(local, totals, points, feature, spread, mask)


def local_tiles(pairs, points, mask):
    count = points.shape[0]
    return pl.pallas_call(
        local_kernel,
        out_shape=[shape(4, count, 128), shape(count, 48, 128, dtype=bf16)],
        in_specs=[in_smem(), in_vmem(), in_vmem()],
        out_specs=[in_vmem()] * 2,
        scratch_shapes=[
            pltpu.VMEM((count, 16, 128), f32),
            pltpu.VMEM((count // 16, 128, 128), f32),
            pltpu.VMEM((2, 4, 256, 256), bf16),
        ],
        compiler_params=params(),
        cost_estimate=cost(4 * 10**9),
        name="local_tiles",
    )(pairs, points, mask)


def per_device(
    positions,
    fields,
    storage,
    velocity,
    send_list,
    remote_local,
    remote_mask,
    local_pairs,
    local_mask,
    migrate_list,
):
    count = positions.shape[0]
    peers = send_list.shape[2]
    sends = send_list[0].transpose(0, 2, 1)
    moves = migrate_list.transpose(0, 2, 1)
    rows_first = positions.transpose(1, 0, 2)
    flat_fields = fields.reshape(count * 4, 128)
    part = shape(peers, 8, 128)
    down, here, up, going, points = pl.pallas_call(
        pack_kernel,
        out_shape=[part, part, part, part, shape(count, 8, 128)],
        in_specs=[anywhere()] * 4,
        out_specs=[in_vmem()] * 5,
        scratch_shapes=[
            pltpu.SMEM(sends.shape, jnp.int32),
            pltpu.SMEM(moves.shape, jnp.int32),
            pltpu.VMEM(rows_first.shape, f32),
            pltpu.VMEM(flat_fields.shape, f32),
            pltpu.SemaphoreType.DMA((4,)),
        ],
        compiler_params=pltpu.CompilerParams(vmem_limit_bytes=60 * 1024 * 1024),
        name="pack",
    )(sends, moves, rows_first, flat_fields)
    down = from_behind(down, "region", -1)
    up = from_behind(up, "region", 1)
    outgoing = pl.pallas_call(
        merge_kernel,
        out_shape=shape(peers, 24, 128),
        in_specs=[in_vmem()] * 4,
        out_specs=in_vmem(),
        compiler_params=params(),
        name="merge",
    )(going, down, here, up)
    points, outgoing = lax.optimization_barrier((points, outgoing))
    spread = lax.all_to_all(outgoing, "bulk", split_axis=0, concat_axis=0, tiled=True)
    totals, feature = local_tiles(local_pairs[0].transpose(1, 0), points, local_mask[0])
    local = remote_local[0].transpose(1, 0)
    mask = remote_mask[0].reshape(-1, remote_mask.shape[3], remote_mask.shape[4])
    totals, down_back, up_back = remote_tiles((0, 2), local, totals, points, feature, spread, mask)
    down_back = from_behind(down_back, "region", 1)
    up_back = from_behind(up_back, "region", -1)
    totals, here_back = remote_tiles((1,), local, totals, points, feature, spread, mask)
    stacked = jnp.stack([down_back, here_back, up_back], axis=1)
    returned = lax.all_to_all(stacked, "bulk", split_axis=0, concat_axis=0, tiled=True)
    new_fields, new_velocity, moving = pl.pallas_call(
        update_kernel,
        out_shape=[shape(count * 4, 128), shape(3, count, 128), shape(peers, 8, 128)],
        in_specs=[in_smem()] * 2 + [in_vmem()] * 5,
        out_specs=[in_vmem()] * 3,
        scratch_shapes=[pltpu.VMEM((count, 4, 128), f32), pltpu.VMEM((count, 8, 128), f32)],
        compiler_params=params(),
        name="update",
    )(sends, moves, totals, returned, flat_fields, velocity.transpose(1, 0, 2), storage)
    late = lax.all_to_all(moving, "bulk", split_axis=0, concat_axis=0, tiled=True)
    arrived = pl.pallas_call(
        arrive_kernel,
        out_shape=shape(11, peers, 128),
        in_specs=[in_vmem()] * 2,
        out_specs=in_vmem(),
        compiler_params=params(),
        name="arrive",
    )(late, spread)
    return (
        new_fields.reshape(count, 4, 128),
        new_velocity.transpose(1, 0, 2),
        arrived.transpose(1, 0, 2),
    )


def solution(mesh):
    spec = lambda rank: P(("region", "bulk"), *([None] * (rank - 1)))
    return jax.shard_map(
        per_device,
        mesh=mesh,
        in_specs=tuple(spec(rank) for rank in (3, 3, 2, 3, 4, 3, 5, 3, 4, 3)),
        out_specs=(spec(3), spec(3), spec(3)),
        check_vma=False,
    )
```

```python
import functools

import jax
import jax.numpy as jnp
from jax import lax
from jax.experimental import pallas as pl
from jax.experimental.pallas import tpu as pltpu
from jax.sharding import PartitionSpec as P

bond_stiff = 0.1
press_gain = 0.05
leak_gain = 0.5
time_step = 0.5
inv_horizon = 0.25
vmem_bytes = 40 * 1024 * 1024
f32 = jnp.float32
bf16 = jnp.bfloat16


def from_behind(shard, axis, by):
    peers = lax.axis_size(axis)
    return lax.ppermute(shard, axis, [(i, (i + by) % peers) for i in range(peers)])


def features(block):
    width = block.shape[1]
    x, p, u = block[0:3], block[3:4], block[4:7]
    one = jnp.ones((1, width), f32)
    rows = jnp.concatenate([x, p, p * x, one, u, one, jnp.zeros((4, width), f32)], axis=0)
    high = rows.astype(bf16)
    rest = rows - high.astype(f32)
    middle = rest.astype(bf16)
    low = (rest - middle.astype(f32)).astype(bf16)
    return jnp.concatenate([high, middle, low], axis=0)


def terms_of(sums, x, p, u):
    mean_gain = 0.5 * press_gain
    out = [
        bond_stiff * (sums[8 + k] - u[k] * sums[11])
        - mean_gain * (p * (sums[k] - x[k] * sums[7]) + (sums[4 + k] - x[k] * sums[3]))
        for k in range(3)
    ]
    out.append(leak_gain * (sums[3] - p * sums[7]))
    return out


def block_rows(ref, first, count, stride):
    return ref[pl.ds(first, count, stride=stride), :]


def turn(blocks, turned_ref):
    for g in range(turned_ref.shape[0]):
        group = jnp.concatenate([blocks(16 * g + n) for n in range(16)], axis=0)
        turned_ref[g] = 0.5 * jnp.transpose(group)


def bond_weights(others, owned, words, bits):
    apart = [others[k] - 0.5 * owned[k : k + 1] for k in range(3)]
    size = apart[0] * apart[0] + 1.0 + (apart[1] * apart[1] + apart[2] * apart[2])
    weight = pltpu.reciprocal(size, approx=True)
    intact = (words & bits) != 0
    high = weight.astype(bf16)
    low = (weight - high.astype(f32)).astype(bf16)
    none = jnp.zeros((128, 128), bf16)
    intact_high = jnp.where(intact, high, none)
    intact_low = jnp.where(intact, low, none)
    return intact_high, high, intact_low, low


def split_sums(product):
    product = product[0:16] + product[16:32] + product[32:48]
    intact, every = product[:, :128], product[:, 128:]
    return jnp.concatenate([every[0:8] - intact[0:8], intact[8:16]], axis=0)


def tile_sums(weights, owned_feature, other_feature):
    intact_high, high, intact_low, low = weights
    by_other = jnp.concatenate(
        [
            jnp.concatenate([intact_high, high], axis=1),
            jnp.concatenate([intact_low, low], axis=1),
        ],
        axis=0,
    )
    on_owned = jnp.dot(
        jnp.concatenate([other_feature, other_feature], axis=1),
        by_other,
        preferred_element_type=f32,
    )
    by_owned = jnp.concatenate(
        [
            jnp.concatenate([intact_high, intact_low], axis=1),
            jnp.concatenate([high, low], axis=1),
        ],
        axis=0,
    )
    on_other = lax.dot_general(
        jnp.concatenate([owned_feature, owned_feature], axis=1),
        by_owned,
        (((1,), (1,)), ((), ())),
        preferred_element_type=f32,
    )
    return split_sums(on_owned), split_sums(on_other)


def tile_loop(
    slots, touch, per_step, owned_of, other_of, other_block, mask_ref, turned_ref, points_ref,
    feature_ref, sums_ref, weights_ref, other_feature_ref, store_other,
):
    bits = jnp.left_shift(1, lax.broadcasted_iota(jnp.int32, (16, 8, 128), 1)).reshape(128, 128)
    steps = slots // per_step

    def weigh(step, half):
        for n in range(per_step):
            slot = step * per_step + n
            other = other_of(slot)
            if other_block is not None:
                other_feature_ref[half, n] = features(other_block(slot))
            turned = turned_ref[other // 16]
            lane = 8 * lax.rem(other, 16)
            others = [
                jnp.take_along_axis(turned, jnp.full((128, 128), lane + k, jnp.int32), axis=1)
                for k in range(3)
            ]
            for e in range(touch):
                tile = slot * touch + e
                owned = owned_of(slot, e)
                words = jnp.concatenate(
                    [mask_ref[tile, pl.ds(j, 8, stride=0), :] for j in range(16)], axis=0
                )
                a, b, c, d = bond_weights(others, points_ref[owned], words, bits)
                at = n * touch + e
                weights_ref[half, at, 0:128, 0:128] = a
                weights_ref[half, at, 0:128, 128:256] = b
                weights_ref[half, at, 128:256, 0:128] = c
                weights_ref[half, at, 128:256, 128:256] = d

    def add_up(step, half):
        for n in range(per_step):
            slot = step * per_step + n
            if other_block is not None:
                feature = other_feature_ref[half, n]
            else:
                feature = feature_ref[other_of(slot)]
            on_other = None
            for e in range(touch):
                owned = owned_of(slot, e)
                kept = weights_ref[half, n * touch + e]
                parts = (kept[:128, :128], kept[:128, 128:], kept[128:, :128], kept[128:, 128:])
                on_owned, more = tile_sums(parts, feature_ref[owned], feature)
                sums_ref[owned] += on_owned
                on_other = more if on_other is None else on_other + more
            store_other(slot, on_other)

    weigh(0, 0)

    def body(k, carry):
        weigh(2 * k + 1, 1)
        add_up(2 * k, 0)
        weigh(2 * k + 2, 0)
        add_up(2 * k + 1, 1)
        return carry

    lax.fori_loop(0, steps // 2 - 1, body, 0)
    weigh(steps - 1, 1)
    add_up(steps - 2, 0)
    add_up(steps - 1, 1)


def owned_terms(sums_ref, points, count):
    rows = sums_ref.reshape(sums_ref.shape[0] * 16, 128)
    return lambda first: terms_of(
        [block_rows(rows, first * 16 + r, count, 16) for r in range(12)],
        [points(r) for r in range(3)],
        points(3),
        [points(4 + r) for r in range(3)],
    )


def fetch(copies):
    for copy in copies:
        copy.start()
    for copy in copies:
        copy.wait()


def pack_kernel(
    sends_any, moves_any, positions_any, fields_any, out_ref, points_ref,
    sends_ref, moves_ref, positions_ref, fields_ref, sems,
):
    pairs = (
        (positions_any, positions_ref),
        (fields_any, fields_ref),
        (sends_any, sends_ref),
        (moves_any, moves_ref),
    )
    fetch([pltpu.make_async_copy(a, b, sems.at[n]) for n, (a, b) in enumerate(pairs)])
    count = positions_ref.shape[1]
    flat = points_ref.reshape(count * 8, 128)
    for k in range(3):
        flat[pl.ds(k, count, stride=8), :] = positions_ref[k]
        flat[pl.ds(4 + k, count, stride=8), :] = block_rows(fields_ref, k, count, 4)
    flat[pl.ds(3, count, stride=8), :] = block_rows(fields_ref, 3, count, 4)
    flat[pl.ds(7, count, stride=8), :] = jnp.zeros((count, 128), f32)
    last = lax.broadcasted_iota(jnp.int32, (8, 128), 0) == 7

    def one_peer(peer, carry):
        move = moves_ref[0, 0, peer]
        moved = points_ref[jnp.maximum(move, 0)]
        moved = jnp.where(move >= 0, moved, jnp.zeros_like(moved))
        for o in range(3):
            block = points_ref[sends_ref[o, 0, peer]]
            out_ref[peer, 8 * o : 8 * o + 8] = jnp.where(last, moved[o : o + 1], block)
        return carry

    lax.fori_loop(0, out_ref.shape[0], one_peer, 0, unroll=8)


def local_kernel(
    pairs_ref, points_ref, mask_ref, totals_ref, feature_ref, sums_ref, turned_ref, weights_ref
):
    count = points_ref.shape[0]
    tiles = mask_ref.shape[0]
    sums_ref[...] = jnp.zeros_like(sums_ref)
    turn(lambda n: points_ref[n], turned_ref)

    def one_block(block, carry):
        feature_ref[block] = features(points_ref[block])
        return carry

    lax.fori_loop(0, count, one_block, 0, unroll=8)

    def store_other(slot, on_other):
        sums_ref[pairs_ref[1, slot]] += on_other

    tile_loop(
        tiles, 1, 4, lambda slot, e: pairs_ref[0, slot], lambda slot: pairs_ref[1, slot], None,
        mask_ref, turned_ref, points_ref, feature_ref, sums_ref, weights_ref, None, store_other,
    )
    flat = points_ref.reshape(count * 8, 128)
    terms = owned_terms(sums_ref, lambda r: block_rows(flat, r, count, 8), count)
    for k, row in enumerate(terms(0)):
        totals_ref[k] = row


def remote_kernel(parts, adds, earlier, local_ref, points_ref, feature_ref, mask_any, *rest):
    sources, rest = rest[: len(parts)], rest[len(parts) :]
    add_refs, rest = rest[:adds], rest[adds:]
    earlier_refs, rest = rest[:earlier], rest[earlier:]
    totals_ref, rest = rest[0], rest[1:]
    back, rest = rest[: len(parts)], rest[len(parts) :]
    (
        sums_ref, turned_ref, weights_ref, other_feature_ref, other_sums, blocks_ref, mask_ref, sems,
    ) = rest
    count = points_ref.shape[0]
    per_part = parts[0][3]
    slots = per_part * len(parts)
    starts = [group * first_of_group + first for group, _, first, _, first_of_group in parts]
    copies = [
        pltpu.make_async_copy(
            mask_any.at[pl.ds(2 * start, 2 * per_part)],
            mask_ref.at[pl.ds(2 * n * per_part, 2 * per_part)],
            sems.at[n],
        )
        for n, start in enumerate(starts)
    ]
    for copy in copies:
        copy.start()
    for n, (_, row, first, _, _) in enumerate(parts):
        for m in range(per_part):
            blocks_ref[n * per_part + m] = sources[n][first + m, row : row + 8]
    turn(lambda n: blocks_ref[n], turned_ref)
    sums_ref[...] = jnp.zeros_like(sums_ref)
    for copy in copies:
        copy.wait()
    gap = starts[-1] - starts[0] - per_part

    def owned_of(slot, e):
        return local_ref[e, slot + starts[0] + gap * (slot // per_part)]

    def store_other(slot, on_other):
        other_sums[slot] = on_other

    tile_loop(
        slots, 2, 2, owned_of, lambda slot: slot, lambda slot: blocks_ref[slot], mask_ref, turned_ref,
        points_ref, feature_ref, sums_ref, weights_ref, other_feature_ref, store_other,
    )
    flat = blocks_ref.reshape(slots * 8, 128)
    for n in range(len(parts)):
        base = n * per_part
        terms = owned_terms(other_sums, lambda r: block_rows(flat, 8 * base + r, per_part, 8), per_part)
        before = back[n].shape[0] - per_part
        if before:
            back[n][0:before] = earlier_refs[n][...]
        rows = back[n].reshape(back[n].shape[0] * 4, 128)
        for k, row in enumerate(terms(base)):
            rows[pl.ds(4 * before + k, per_part, stride=4), :] = row
    own = points_ref.reshape(count * 8, 128)
    terms = owned_terms(sums_ref, lambda r: block_rows(own, r, count, 8), count)
    for k, row in enumerate(terms(0)):
        for add in add_refs:
            row = row + add[k]
        totals_ref[k] = row


def update_kernel(
    sends_ref, moves_ref, totals_ref, returned_ref, fields_ref, velocity_ref, storage_ref,
    new_fields_ref, new_velocity_ref, moving_ref, sums_ref, rows_ref,
):
    count = storage_ref.shape[0]
    peers = returned_ref.shape[0]
    sums_ref[...] = jnp.zeros_like(sums_ref)

    def one_peer(peer, carry):
        for o in range(3):
            sums_ref[sends_ref[o, 0, peer]] += returned_ref[peer, o]
        return carry

    lax.fori_loop(0, peers, one_peer, 0, unroll=4)
    sums = sums_ref.reshape(count * 4, 128)
    rows = rows_ref.reshape(count * 8, 128)
    for k in range(3):
        speed = velocity_ref[k] + time_step * (totals_ref[k] + block_rows(sums, k, count, 4))
        moved = block_rows(fields_ref, k, count, 4) + time_step * speed
        new_velocity_ref[k] = speed
        new_fields_ref[pl.ds(k, count, stride=4), :] = moved
        rows[pl.ds(k, count, stride=8), :] = moved
        rows[pl.ds(4 + k, count, stride=8), :] = speed
    stored = storage_ref[...]
    pressure = (
        block_rows(fields_ref, 3, count, 4)
        + time_step * (totals_ref[3] + block_rows(sums, 3, count, 4)) / stored
    )
    new_fields_ref[pl.ds(3, count, stride=4), :] = pressure
    rows[pl.ds(3, count, stride=8), :] = pressure
    rows[pl.ds(7, count, stride=8), :] = stored

    def one_move(peer, carry):
        move = moves_ref[0, 0, peer]
        block = rows_ref[jnp.maximum(move, 0)]
        moving_ref[peer] = jnp.where(move >= 0, block, jnp.zeros_like(block))
        return carry

    lax.fori_loop(0, peers, one_move, 0, unroll=4)


def arrive_kernel(late_ref, early_ref, out_ref):
    peers = late_ref.shape[0]
    late = late_ref.reshape(peers * 8, 128)
    early = early_ref.reshape(peers * 24, 128)
    for k in range(7):
        out_ref[k] = block_rows(late, k, peers, 8)
    for k in range(3):
        out_ref[7 + k] = block_rows(early, 8 * k + 7, peers, 24)
    out_ref[10] = block_rows(late, 7, peers, 8)


def in_vmem():
    return pl.BlockSpec(memory_space=pltpu.VMEM)


def in_smem():
    return pl.BlockSpec(memory_space=pltpu.SMEM)


def params():
    return pltpu.CompilerParams(vmem_limit_bytes=vmem_bytes)


def cost(flops):
    return pl.CostEstimate(flops=flops, bytes_accessed=2 * 1024 * 1024, transcendentals=0)


def shape(*dims, dtype=f32):
    return jax.ShapeDtypeStruct(dims, dtype)


def anywhere():
    return pl.BlockSpec(memory_space=pl.ANY)


def remote_tiles(parts, local, points, feature, mask, sources, adds=(), earlier=()):
    count = points.shape[0]
    per_part = parts[0][3]
    slots = per_part * len(parts)
    before = earlier[0].shape[0] if earlier else 0
    return pl.pallas_call(
        functools.partial(remote_kernel, parts, len(adds), len(earlier)),
        out_shape=[shape(4, count, 128)] + [shape(before + per_part, 4, 128)] * len(parts),
        in_specs=[in_smem(), in_vmem(), in_vmem(), anywhere()]
        + [in_vmem()] * (len(sources) + len(adds) + len(earlier)),
        out_specs=[in_vmem()] * (1 + len(parts)),
        scratch_shapes=[
            pltpu.VMEM((count, 16, 128), f32),
            pltpu.VMEM((slots // 16, 128, 128), f32),
            pltpu.VMEM((2, 4, 256, 256), bf16),
            pltpu.VMEM((2, 2, 48, 128), bf16),
            pltpu.VMEM((slots, 16, 128), f32),
            pltpu.VMEM((slots, 8, 128), f32),
            pltpu.VMEM((2 * slots, 16, 128), jnp.int32),
            pltpu.SemaphoreType.DMA((len(parts),)),
        ],
        compiler_params=params(),
        cost_estimate=cost(slots * 10**8),
        name="remote_tiles",
    )(local, points, feature, mask, *sources, *adds, *earlier)


def local_tiles(pairs, points, mask):
    count = points.shape[0]
    return pl.pallas_call(
        local_kernel,
        out_shape=[shape(4, count, 128), shape(count, 48, 128, dtype=bf16)],
        in_specs=[in_smem(), in_vmem(), in_vmem()],
        out_specs=[in_vmem()] * 2,
        scratch_shapes=[
            pltpu.VMEM((count, 16, 128), f32),
            pltpu.VMEM((count // 16, 128, 128), f32),
            pltpu.VMEM((2, 4, 256, 256), bf16),
        ],
        compiler_params=params(),
        cost_estimate=cost(4 * 10**9),
        name="local_tiles",
    )(pairs, points, mask)


def per_device(
    positions,
    fields,
    storage,
    velocity,
    send_list,
    remote_local,
    remote_mask,
    local_pairs,
    local_mask,
    migrate_list,
):
    count = positions.shape[0]
    peers = send_list.shape[2]
    sends = send_list[0].transpose(0, 2, 1)
    moves = migrate_list.transpose(0, 2, 1)
    rows_first = positions.transpose(1, 0, 2)
    flat_fields = fields.reshape(count * 4, 128)
    outgoing, points = pl.pallas_call(
        pack_kernel,
        out_shape=[shape(peers, 24, 128), shape(count, 8, 128)],
        in_specs=[anywhere()] * 4,
        out_specs=[in_vmem()] * 2,
        scratch_shapes=[
            pltpu.SMEM(sends.shape, jnp.int32),
            pltpu.SMEM(moves.shape, jnp.int32),
            pltpu.VMEM(rows_first.shape, f32),
            pltpu.VMEM(flat_fields.shape, f32),
            pltpu.SemaphoreType.DMA((4,)),
        ],
        compiler_params=pltpu.CompilerParams(vmem_limit_bytes=60 * 1024 * 1024),
        name="pack",
    )(sends, moves, rows_first, flat_fields)
    spread = lax.all_to_all(outgoing, "bulk", split_axis=0, concat_axis=0, tiled=True)
    local_totals, feature = local_tiles(local_pairs[0].transpose(1, 0), points, local_mask[0])
    spread, feature = lax.optimization_barrier((spread, feature))
    local = remote_local[0].transpose(1, 0)
    mask = remote_mask[0].reshape(-1, remote_mask.shape[3], remote_mask.shape[4])
    tile_args = (local, points, feature, mask)
    down = from_behind(spread[:, 0:8], "region", -1)
    up = from_behind(spread[:, 16:24], "region", 1)
    half = peers // 2
    first_totals, first_back = remote_tiles(((1, 8, 0, half, peers),), *tile_args, [spread])
    far_totals, down_back, up_back = remote_tiles(
        ((0, 0, 0, peers, peers), (2, 0, 0, peers, peers)), *tile_args, [down, up]
    )
    down_back = from_behind(down_back, "region", 1)
    up_back = from_behind(up_back, "region", -1)
    totals, here_back = remote_tiles(
        ((1, 8, half, half, peers),), *tile_args, [spread],
        [local_totals, first_totals, far_totals], [first_back],
    )
    stacked = jnp.stack([down_back, here_back, up_back], axis=1)
    returned = lax.all_to_all(stacked, "bulk", split_axis=0, concat_axis=0, tiled=True)
    new_fields, new_velocity, moving = pl.pallas_call(
        update_kernel,
        out_shape=[shape(count * 4, 128), shape(3, count, 128), shape(peers, 8, 128)],
        in_specs=[in_smem()] * 2 + [in_vmem()] * 5,
        out_specs=[in_vmem()] * 3,
        scratch_shapes=[pltpu.VMEM((count, 4, 128), f32), pltpu.VMEM((count, 8, 128), f32)],
        compiler_params=params(),
        name="update",
    )(sends, moves, totals, returned, flat_fields, velocity.transpose(1, 0, 2), storage)
    late = lax.all_to_all(moving, "bulk", split_axis=0, concat_axis=0, tiled=True)
    arrived = pl.pallas_call(
        arrive_kernel,
        out_shape=shape(11, peers, 128),
        in_specs=[in_vmem()] * 2,
        out_specs=in_vmem(),
        compiler_params=params(),
        name="arrive",
    )(late, spread)
    return (
        new_fields.reshape(count, 4, 128),
        new_velocity.transpose(1, 0, 2),
        arrived.transpose(1, 0, 2),
    )


def solution(mesh):
    spec = lambda rank: P(("region", "bulk"), *([None] * (rank - 1)))
    return jax.shard_map(
        per_device,
        mesh=mesh,
        in_specs=tuple(spec(rank) for rank in (3, 3, 2, 3, 4, 3, 5, 3, 4, 3)),
        out_specs=(spec(3), spec(3), spec(3)),
        check_vma=False,
    )
```

```python
import functools

import jax
import jax.numpy as jnp
from jax import lax
from jax.experimental import pallas as pl
from jax.experimental.pallas import tpu as pltpu
from jax.sharding import PartitionSpec as P

bond_stiff = 0.1
press_gain = 0.05
leak_gain = 0.5
time_step = 0.5
inv_horizon = 0.25
vmem_bytes = 40 * 1024 * 1024
f32 = jnp.float32
bf16 = jnp.bfloat16


def from_behind(shard, axis, by):
    peers = lax.axis_size(axis)
    return lax.ppermute(shard, axis, [(i, (i + by) % peers) for i in range(peers)])


def features(block):
    width = block.shape[1]
    x, p, u = block[0:3], block[3:4], block[4:7]
    one = jnp.ones((1, width), f32)
    rows = jnp.concatenate([x, p, p * x, one, u, one, jnp.zeros((4, width), f32)], axis=0)
    high = rows.astype(bf16)
    rest = rows - high.astype(f32)
    middle = rest.astype(bf16)
    low = (rest - middle.astype(f32)).astype(bf16)
    return jnp.concatenate([high, middle, low], axis=0)


def terms_of(sums, x, p, u):
    mean_gain = 0.5 * press_gain
    out = [
        bond_stiff * (sums[8 + k] - u[k] * sums[11])
        - mean_gain * (p * (sums[k] - x[k] * sums[7]) + (sums[4 + k] - x[k] * sums[3]))
        for k in range(3)
    ]
    out.append(leak_gain * (sums[3] - p * sums[7]))
    return out


def block_rows(ref, first, count, stride):
    return ref[pl.ds(first, count, stride=stride), :]


def turn(blocks, turned_ref):
    for g in range(turned_ref.shape[0]):
        group = jnp.concatenate([blocks(16 * g + n) for n in range(16)], axis=0)
        turned_ref[g] = 0.5 * jnp.transpose(group)


def bond_weights(others, owned, words, bits):
    apart = [others[k] - 0.5 * owned[k : k + 1] for k in range(3)]
    size = apart[0] * apart[0] + 1.0 + (apart[1] * apart[1] + apart[2] * apart[2])
    weight = pltpu.reciprocal(size, approx=True)
    intact = (words & bits) != 0
    high = weight.astype(bf16)
    low = (weight - high.astype(f32)).astype(bf16)
    none = jnp.zeros((128, 128), bf16)
    intact_high = jnp.where(intact, high, none)
    intact_low = jnp.where(intact, low, none)
    return intact_high, high, intact_low, low


def split_sums(product):
    product = product[0:16] + product[16:32] + product[32:48]
    intact, every = product[:, :128], product[:, 128:]
    return jnp.concatenate([every[0:8] - intact[0:8], intact[8:16]], axis=0)


def tile_sums(weights, owned_feature, other_feature):
    intact_high, high, intact_low, low = weights
    by_other = jnp.concatenate(
        [
            jnp.concatenate([intact_high, high], axis=1),
            jnp.concatenate([intact_low, low], axis=1),
        ],
        axis=0,
    )
    on_owned = jnp.dot(
        jnp.concatenate([other_feature, other_feature], axis=1),
        by_other,
        preferred_element_type=f32,
    )
    by_owned = jnp.concatenate(
        [
            jnp.concatenate([intact_high, intact_low], axis=1),
            jnp.concatenate([high, low], axis=1),
        ],
        axis=0,
    )
    on_other = lax.dot_general(
        jnp.concatenate([owned_feature, owned_feature], axis=1),
        by_owned,
        (((1,), (1,)), ((), ())),
        preferred_element_type=f32,
    )
    return split_sums(on_owned), split_sums(on_other)


def tile_loop(
    slots, touch, per_step, owned_of, other_of, other_block, words_of, turned_ref, points_ref,
    feature_ref, sums_ref, weights_ref, other_feature_ref, store_other,
):
    bits = jnp.left_shift(1, lax.broadcasted_iota(jnp.int32, (16, 8, 128), 1)).reshape(128, 128)
    steps = slots // per_step

    def weigh(step, half):
        for n in range(per_step):
            slot = step * per_step + n
            other = other_of(slot)
            if other_block is not None:
                other_feature_ref[half, n] = features(other_block(slot))
            turned = turned_ref[other // 16]
            lane = 8 * lax.rem(other, 16)
            others = [
                jnp.take_along_axis(turned, jnp.full((128, 128), lane + k, jnp.int32), axis=1)
                for k in range(3)
            ]
            for e in range(touch):
                owned = owned_of(slot, e)
                a, b, c, d = bond_weights(others, points_ref[owned], words_of(slot, e), bits)
                at = n * touch + e
                weights_ref[half, at, 0:128, 0:128] = a
                weights_ref[half, at, 0:128, 128:256] = b
                weights_ref[half, at, 128:256, 0:128] = c
                weights_ref[half, at, 128:256, 128:256] = d

    def add_up(step, half):
        for n in range(per_step):
            slot = step * per_step + n
            if other_block is not None:
                feature = other_feature_ref[half, n]
            else:
                feature = feature_ref[other_of(slot)]
            on_other = None
            for e in range(touch):
                owned = owned_of(slot, e)
                kept = weights_ref[half, n * touch + e]
                parts = (kept[:128, :128], kept[:128, 128:], kept[128:, :128], kept[128:, 128:])
                on_owned, more = tile_sums(parts, feature_ref[owned], feature)
                sums_ref[owned] += on_owned
                on_other = more if on_other is None else on_other + more
            store_other(slot, on_other)

    weigh(0, 0)

    def body(k, carry):
        weigh(2 * k + 1, 1)
        add_up(2 * k, 0)
        weigh(2 * k + 2, 0)
        add_up(2 * k + 1, 1)
        return carry

    lax.fori_loop(0, steps // 2 - 1, body, 0)
    weigh(steps - 1, 1)
    add_up(steps - 2, 0)
    add_up(steps - 1, 1)


def block_terms(sums_ref, first, blocks_ref, count, put):
    sums = sums_ref.reshape(sums_ref.shape[0] * 16, 128)
    rows = blocks_ref.reshape(blocks_ref.shape[0] * 8, 128)
    for n in range(0, count, 16):
        own = [block_rows(rows, 8 * (first + n) + r, 16, 8) for r in range(7)]
        terms = terms_of(
            [block_rows(sums, 16 * (first + n) + r, 16, 16) for r in range(12)],
            own[0:3],
            own[3],
            own[4:7],
        )
        for k, row in enumerate(terms):
            put(k, n, row)


def fetch(copies):
    for copy in copies:
        copy.start()
    for copy in copies:
        copy.wait()


def pack_kernel(
    sends_any, moves_any, positions_any, fields_any, out_ref, points_ref,
    sends_ref, moves_ref, positions_ref, fields_ref, sems,
):
    pairs = (
        (positions_any, positions_ref),
        (fields_any, fields_ref),
        (sends_any, sends_ref),
        (moves_any, moves_ref),
    )
    fetch([pltpu.make_async_copy(a, b, sems.at[n]) for n, (a, b) in enumerate(pairs)])
    count = positions_ref.shape[1]
    flat = points_ref.reshape(count * 8, 128)
    for k in range(3):
        flat[pl.ds(k, count, stride=8), :] = positions_ref[k]
        flat[pl.ds(4 + k, count, stride=8), :] = block_rows(fields_ref, k, count, 4)
    flat[pl.ds(3, count, stride=8), :] = block_rows(fields_ref, 3, count, 4)
    flat[pl.ds(7, count, stride=8), :] = jnp.zeros((count, 128), f32)
    last = lax.broadcasted_iota(jnp.int32, (8, 128), 0) == 7

    def one_peer(peer, carry):
        move = moves_ref[0, 0, peer]
        moved = points_ref[jnp.maximum(move, 0)]
        moved = jnp.where(move >= 0, moved, jnp.zeros_like(moved))
        for o in range(3):
            block = points_ref[sends_ref[o, 0, peer]]
            out_ref[peer, 8 * o : 8 * o + 8] = jnp.where(last, moved[o : o + 1], block)
        return carry

    lax.fori_loop(0, out_ref.shape[0], one_peer, 0, unroll=8)


def local_kernel(
    pairs_ref, points_ref, mask_ref, totals_ref, feature_ref, sums_ref, turned_ref, weights_ref
):
    count = points_ref.shape[0]
    tiles = mask_ref.shape[0]
    sums_ref[...] = jnp.zeros_like(sums_ref)
    turn(lambda n: points_ref[n], turned_ref)

    def one_block(block, carry):
        feature_ref[block] = features(points_ref[block])
        return carry

    lax.fori_loop(0, count, one_block, 0, unroll=8)

    def words_of(slot, e):
        return jnp.concatenate([mask_ref[slot, pl.ds(j, 8, stride=0), :] for j in range(16)], axis=0)

    def store_other(slot, on_other):
        sums_ref[pairs_ref[1, slot]] += on_other

    tile_loop(
        tiles, 1, 4, lambda slot, e: pairs_ref[0, slot], lambda slot: pairs_ref[1, slot], None,
        words_of, turned_ref, points_ref, feature_ref, sums_ref, weights_ref, None, store_other,
    )

    def put(k, n, row):
        totals_ref[k, n : n + 16] = row

    block_terms(sums_ref, 0, points_ref, count, put)


def remote_kernel(parts, adds, earlier, local_ref, points_ref, feature_ref, mask_ref, *rest):
    sources, rest = rest[: len(parts)], rest[len(parts) :]
    add_refs, rest = rest[:adds], rest[adds:]
    earlier_refs, rest = rest[:earlier], rest[earlier:]
    totals_ref, rest = rest[0], rest[1:]
    back, rest = rest[: len(parts)], rest[len(parts) :]
    sums_ref, turned_ref, weights_ref, other_feature_ref, other_sums, blocks_ref = rest
    count = points_ref.shape[0]
    per_part = parts[0][3]
    slots = per_part * len(parts)
    starts = [group * first_of_group + first for group, _, first, _, first_of_group in parts]
    for n, (_, row, first, _, _) in enumerate(parts):
        for m in range(per_part):
            blocks_ref[n * per_part + m] = sources[n][first + m, row : row + 8]
    turn(lambda n: blocks_ref[n], turned_ref)
    sums_ref[...] = jnp.zeros_like(sums_ref)
    gap = starts[-1] - starts[0] - per_part

    def entry(slot):
        return slot + starts[0] + gap * (slot // per_part)

    def owned_of(slot, e):
        return local_ref[e, entry(slot)]

    def words_of(slot, e):
        tile = 2 * entry(slot) + e
        return jnp.concatenate([mask_ref[tile, pl.ds(j, 8, stride=0), :] for j in range(16)], axis=0)

    def store_other(slot, on_other):
        other_sums[slot] = on_other

    tile_loop(
        slots, 2, 2, owned_of, lambda slot: slot, lambda slot: blocks_ref[slot], words_of, turned_ref,
        points_ref, feature_ref, sums_ref, weights_ref, other_feature_ref, store_other,
    )
    for part in range(len(parts)):
        before = back[part].shape[0] - per_part
        if before:
            back[part][0:before] = earlier_refs[part][...]
        rows = back[part].reshape(back[part].shape[0] * 4, 128)

        def put_back(k, n, row):
            rows[pl.ds(4 * (before + n) + k, 16, stride=4), :] = row

        block_terms(other_sums, part * per_part, blocks_ref, per_part, put_back)

    def put(k, n, row):
        for add in add_refs:
            row = row + add[k, n : n + 16]
        totals_ref[k, n : n + 16] = row

    block_terms(sums_ref, 0, points_ref, count, put)


def update_kernel(
    sends_ref, moves_ref, totals_ref, returned_ref, fields_ref, velocity_ref, storage_ref,
    new_fields_ref, new_velocity_ref, moving_ref, down_ref, here_ref, up_ref, rows_ref,
):
    count = storage_ref.shape[0]
    peers = returned_ref.shape[0]
    sums_refs = (down_ref, here_ref, up_ref)
    for sums_ref in sums_refs:
        sums_ref[...] = jnp.zeros_like(sums_ref)

    def one_peer(peer, carry):
        for o, sums_ref in enumerate(sums_refs):
            sums_ref[sends_ref[o, 0, peer]] += returned_ref[peer, o]
        return carry

    lax.fori_loop(0, peers, one_peer, 0, unroll=8)
    flats = [sums_ref.reshape(count * 4, 128) for sums_ref in sums_refs]

    def total(k):
        down, here, up = (block_rows(flat, k, count, 4) for flat in flats)
        return totals_ref[k] + (down + here + up)

    rows = rows_ref.reshape(count * 8, 128)
    for k in range(3):
        speed = velocity_ref[k] + time_step * total(k)
        moved = block_rows(fields_ref, k, count, 4) + time_step * speed
        new_velocity_ref[k] = speed
        new_fields_ref[pl.ds(k, count, stride=4), :] = moved
        rows[pl.ds(k, count, stride=8), :] = moved
        rows[pl.ds(4 + k, count, stride=8), :] = speed
    stored = storage_ref[...]
    pressure = (
        block_rows(fields_ref, 3, count, 4)
        + time_step * total(3) / stored
    )
    new_fields_ref[pl.ds(3, count, stride=4), :] = pressure
    rows[pl.ds(3, count, stride=8), :] = pressure
    rows[pl.ds(7, count, stride=8), :] = stored

    def one_move(peer, carry):
        move = moves_ref[0, 0, peer]
        block = rows_ref[jnp.maximum(move, 0)]
        moving_ref[peer] = jnp.where(move >= 0, block, jnp.zeros_like(block))
        return carry

    lax.fori_loop(0, peers, one_move, 0, unroll=4)


def arrive_kernel(late_ref, early_ref, out_ref):
    peers = late_ref.shape[0]
    late = late_ref.reshape(peers * 8, 128)
    early = early_ref.reshape(peers * 24, 128)
    for k in range(7):
        out_ref[k] = block_rows(late, k, peers, 8)
    for k in range(3):
        out_ref[7 + k] = block_rows(early, 8 * k + 7, peers, 24)
    out_ref[10] = block_rows(late, 7, peers, 8)


def in_vmem():
    return pl.BlockSpec(memory_space=pltpu.VMEM)


def in_smem():
    return pl.BlockSpec(memory_space=pltpu.SMEM)


def params():
    return pltpu.CompilerParams(vmem_limit_bytes=vmem_bytes)


def cost(flops):
    return pl.CostEstimate(flops=flops, bytes_accessed=2 * 1024 * 1024, transcendentals=0)


def shape(*dims, dtype=f32):
    return jax.ShapeDtypeStruct(dims, dtype)


def anywhere():
    return pl.BlockSpec(memory_space=pl.ANY)


def remote_tiles(parts, local, points, feature, mask, sources, adds=(), earlier=()):
    count = points.shape[0]
    per_part = parts[0][3]
    slots = per_part * len(parts)
    before = earlier[0].shape[0] if earlier else 0
    return pl.pallas_call(
        functools.partial(remote_kernel, parts, len(adds), len(earlier)),
        out_shape=[shape(4, count, 128)] + [shape(before + per_part, 4, 128)] * len(parts),
        in_specs=[in_smem()] + [in_vmem()] * (3 + len(sources) + len(adds) + len(earlier)),
        out_specs=[in_vmem()] * (1 + len(parts)),
        scratch_shapes=[
            pltpu.VMEM((count, 16, 128), f32),
            pltpu.VMEM((slots // 16, 128, 128), f32),
            pltpu.VMEM((2, 4, 256, 256), bf16),
            pltpu.VMEM((2, 2, 48, 128), bf16),
            pltpu.VMEM((slots, 16, 128), f32),
            pltpu.VMEM((slots, 8, 128), f32),
        ],
        compiler_params=params(),
        cost_estimate=cost(slots * 10**8),
        name="remote_tiles",
    )(local, points, feature, mask, *sources, *adds, *earlier)


def local_tiles(pairs, points, mask):
    count = points.shape[0]
    return pl.pallas_call(
        local_kernel,
        out_shape=[shape(4, count, 128), shape(count, 48, 128, dtype=bf16)],
        in_specs=[in_smem(), in_vmem(), in_vmem()],
        out_specs=[in_vmem()] * 2,
        scratch_shapes=[
            pltpu.VMEM((count, 16, 128), f32),
            pltpu.VMEM((count // 16, 128, 128), f32),
            pltpu.VMEM((2, 4, 256, 256), bf16),
        ],
        compiler_params=params(),
        cost_estimate=cost(4 * 10**9),
        name="local_tiles",
    )(pairs, points, mask)


def per_device(
    positions,
    fields,
    storage,
    velocity,
    send_list,
    remote_local,
    remote_mask,
    local_pairs,
    local_mask,
    migrate_list,
):
    count = positions.shape[0]
    peers = send_list.shape[2]
    sends = send_list[0].transpose(0, 2, 1)
    moves = migrate_list.transpose(0, 2, 1)
    rows_first = positions.transpose(1, 0, 2)
    flat_fields = fields.reshape(count * 4, 128)
    outgoing, points = pl.pallas_call(
        pack_kernel,
        out_shape=[shape(peers, 24, 128), shape(count, 8, 128)],
        in_specs=[anywhere()] * 4,
        out_specs=[in_vmem()] * 2,
        scratch_shapes=[
            pltpu.SMEM(sends.shape, jnp.int32),
            pltpu.SMEM(moves.shape, jnp.int32),
            pltpu.VMEM(rows_first.shape, f32),
            pltpu.VMEM(flat_fields.shape, f32),
            pltpu.SemaphoreType.DMA((4,)),
        ],
        compiler_params=pltpu.CompilerParams(vmem_limit_bytes=60 * 1024 * 1024),
        name="pack",
    )(sends, moves, rows_first, flat_fields)
    spread = lax.all_to_all(outgoing, "bulk", split_axis=0, concat_axis=0, tiled=True)
    local_totals, feature = local_tiles(local_pairs[0].transpose(1, 0), points, local_mask[0])
    spread, feature = lax.optimization_barrier((spread, feature))
    local = remote_local[0].transpose(1, 0)
    mask = remote_mask[0].reshape(-1, remote_mask.shape[3], remote_mask.shape[4])
    tile_args = (local, points, feature, mask)
    down = from_behind(spread[:, 0:8], "region", -1)
    up = from_behind(spread[:, 16:24], "region", 1)
    half = peers // 2
    first_totals, first_back = remote_tiles(((1, 8, 0, half, peers),), *tile_args, [spread])
    far_totals, down_back, up_back = remote_tiles(
        ((0, 0, 0, peers, peers), (2, 0, 0, peers, peers)), *tile_args, [down, up]
    )
    down_back = from_behind(down_back, "region", 1)
    up_back = from_behind(up_back, "region", -1)
    totals, here_back = remote_tiles(
        ((1, 8, half, half, peers),), *tile_args, [spread],
        [local_totals, first_totals, far_totals], [first_back],
    )
    stacked = jnp.stack([down_back, here_back, up_back], axis=1)
    returned = lax.all_to_all(stacked, "bulk", split_axis=0, concat_axis=0, tiled=True)
    new_fields, new_velocity, moving = pl.pallas_call(
        update_kernel,
        out_shape=[shape(count * 4, 128), shape(3, count, 128), shape(peers, 8, 128)],
        in_specs=[in_smem()] * 2 + [in_vmem()] * 5,
        out_specs=[in_vmem()] * 3,
        scratch_shapes=[pltpu.VMEM((count, 4, 128), f32)] * 3 + [pltpu.VMEM((count, 8, 128), f32)],
        compiler_params=params(),
        name="update",
    )(sends, moves, totals, returned, flat_fields, velocity.transpose(1, 0, 2), storage)
    late = lax.all_to_all(moving, "bulk", split_axis=0, concat_axis=0, tiled=True)
    arrived = pl.pallas_call(
        arrive_kernel,
        out_shape=shape(11, peers, 128),
        in_specs=[in_vmem()] * 2,
        out_specs=in_vmem(),
        compiler_params=params(),
        name="arrive",
    )(late, spread)
    return (
        new_fields.reshape(count, 4, 128),
        new_velocity.transpose(1, 0, 2),
        arrived.transpose(1, 0, 2),
    )


def solution(mesh):
    spec = lambda rank: P(("region", "bulk"), *([None] * (rank - 1)))
    return jax.shard_map(
        per_device,
        mesh=mesh,
        in_specs=tuple(spec(rank) for rank in (3, 3, 2, 3, 4, 3, 5, 3, 4, 3)),
        out_specs=(spec(3), spec(3), spec(3)),
        check_vma=False,
    )
```

```python
import functools

import jax
import jax.numpy as jnp
from jax import lax
from jax.experimental import pallas as pl
from jax.experimental.pallas import tpu as pltpu
from jax.sharding import PartitionSpec as P

bond_stiff = 0.1
press_gain = 0.05
leak_gain = 0.5
time_step = 0.5
inv_horizon = 0.25
vmem_bytes = 40 * 1024 * 1024
f32 = jnp.float32
bf16 = jnp.bfloat16


def from_behind(shard, axis, by):
    peers = lax.axis_size(axis)
    return lax.ppermute(shard, axis, [(i, (i + by) % peers) for i in range(peers)])


def features(block):
    width = block.shape[1]
    x, p, u = block[0:3], block[3:4], block[4:7]
    one = jnp.ones((1, width), f32)
    rows = jnp.concatenate([x, p, p * x, one, u, one, jnp.zeros((4, width), f32)], axis=0)
    high = rows.astype(bf16)
    rest = rows - high.astype(f32)
    middle = rest.astype(bf16)
    low = (rest - middle.astype(f32)).astype(bf16)
    return jnp.concatenate([high, middle, low], axis=0)


def terms_of(sums, x, p, u):
    mean_gain = 0.5 * press_gain
    out = [
        bond_stiff * (sums[8 + k] - u[k] * sums[11])
        - mean_gain * (p * (sums[k] - x[k] * sums[7]) + (sums[4 + k] - x[k] * sums[3]))
        for k in range(3)
    ]
    out.append(leak_gain * (sums[3] - p * sums[7]))
    return out


def block_rows(ref, first, count, stride):
    return ref[pl.ds(first, count, stride=stride), :]


def turn(blocks, turned_ref):
    for g in range(turned_ref.shape[0]):
        group = jnp.concatenate([blocks(16 * g + n) for n in range(16)], axis=0)
        turned_ref[g] = 0.5 * jnp.transpose(group)


def bond_weights(others, owned, words, bits):
    apart = [others[k] - 0.5 * owned[k : k + 1] for k in range(3)]
    size = apart[0] * apart[0] + 1.0 + (apart[1] * apart[1] + apart[2] * apart[2])
    weight = pltpu.reciprocal(size, approx=True)
    intact = (words & bits) != 0
    high = weight.astype(bf16)
    low = (weight - high.astype(f32)).astype(bf16)
    none = jnp.zeros((128, 128), bf16)
    intact_high = jnp.where(intact, high, none)
    intact_low = jnp.where(intact, low, none)
    return intact_high, high, intact_low, low


def split_sums(product):
    product = product[0:16] + product[16:32] + product[32:48]
    intact, every = product[:, :128], product[:, 128:]
    return jnp.concatenate([every[0:8] - intact[0:8], intact[8:16]], axis=0)


def tile_sums(weights, owned_feature, other_feature):
    intact_high, high, intact_low, low = weights
    by_other = jnp.concatenate(
        [
            jnp.concatenate([intact_high, high], axis=1),
            jnp.concatenate([intact_low, low], axis=1),
        ],
        axis=0,
    )
    on_owned = jnp.dot(
        jnp.concatenate([other_feature, other_feature], axis=1),
        by_other,
        preferred_element_type=f32,
    )
    by_owned = jnp.concatenate(
        [
            jnp.concatenate([intact_high, intact_low], axis=1),
            jnp.concatenate([high, low], axis=1),
        ],
        axis=0,
    )
    on_other = lax.dot_general(
        jnp.concatenate([owned_feature, owned_feature], axis=1),
        by_owned,
        (((1,), (1,)), ((), ())),
        preferred_element_type=f32,
    )
    return split_sums(on_owned), split_sums(on_other)


def tile_loop(
    slots, touch, per_step, owned_of, other_of, other_block, words_of, turned_ref, points_ref,
    feature_ref, sums_ref, weights_ref, other_feature_ref, store_other,
):
    bits = jnp.left_shift(1, lax.broadcasted_iota(jnp.int32, (16, 8, 128), 1)).reshape(128, 128)
    steps = slots // per_step

    def weigh(step, half):
        for n in range(per_step):
            slot = step * per_step + n
            other = other_of(slot)
            if other_block is not None:
                other_feature_ref[half, n] = features(other_block(slot))
            turned = turned_ref[other // 16]
            lane = 8 * lax.rem(other, 16)
            others = [
                jnp.take_along_axis(turned, jnp.full((128, 128), lane + k, jnp.int32), axis=1)
                for k in range(3)
            ]
            for e in range(touch):
                owned = owned_of(slot, e)
                a, b, c, d = bond_weights(others, points_ref[owned], words_of(slot, e), bits)
                at = n * touch + e
                weights_ref[half, at, 0:128, 0:128] = a
                weights_ref[half, at, 0:128, 128:256] = b
                weights_ref[half, at, 128:256, 0:128] = c
                weights_ref[half, at, 128:256, 128:256] = d

    def add_up(step, half):
        for n in range(per_step):
            slot = step * per_step + n
            if other_block is not None:
                feature = other_feature_ref[half, n]
            else:
                feature = feature_ref[other_of(slot)]
            on_other = None
            for e in range(touch):
                owned = owned_of(slot, e)
                kept = weights_ref[half, n * touch + e]
                parts = (kept[:128, :128], kept[:128, 128:], kept[128:, :128], kept[128:, 128:])
                on_owned, more = tile_sums(parts, feature_ref[owned], feature)
                sums_ref[owned] += on_owned
                on_other = more if on_other is None else on_other + more
            store_other(slot, on_other)

    weigh(0, 0)

    def body(k, carry):
        for n in range(4):
            weigh(4 * k + n + 1, (n + 1) % 4)
            add_up(4 * k + n, n)
        return carry

    lax.fori_loop(0, steps // 4 - 1, body, 0)
    for n in range(4):
        if n < 3:
            weigh(steps - 3 + n, n + 1)
        add_up(steps - 4 + n, n)


def block_terms(sums_ref, first, blocks_ref, count, put):
    sums = sums_ref.reshape(sums_ref.shape[0] * 16, 128)
    rows = blocks_ref.reshape(blocks_ref.shape[0] * 8, 128)
    for n in range(0, count, 16):
        own = [block_rows(rows, 8 * (first + n) + r, 16, 8) for r in range(7)]
        terms = terms_of(
            [block_rows(sums, 16 * (first + n) + r, 16, 16) for r in range(12)],
            own[0:3],
            own[3],
            own[4:7],
        )
        for k, row in enumerate(terms):
            put(k, n, row)


def fetch(copies):
    for copy in copies:
        copy.start()
    for copy in copies:
        copy.wait()


def pack_kernel(
    sends_any, moves_any, positions_any, fields_any, out_ref, points_ref,
    sends_ref, moves_ref, positions_ref, fields_ref, sems,
):
    pairs = (
        (positions_any, positions_ref),
        (fields_any, fields_ref),
        (sends_any, sends_ref),
        (moves_any, moves_ref),
    )
    fetch([pltpu.make_async_copy(a, b, sems.at[n]) for n, (a, b) in enumerate(pairs)])
    count = positions_ref.shape[1]
    flat = points_ref.reshape(count * 8, 128)
    for k in range(3):
        flat[pl.ds(k, count, stride=8), :] = positions_ref[k]
        flat[pl.ds(4 + k, count, stride=8), :] = block_rows(fields_ref, k, count, 4)
    flat[pl.ds(3, count, stride=8), :] = block_rows(fields_ref, 3, count, 4)
    flat[pl.ds(7, count, stride=8), :] = jnp.zeros((count, 128), f32)
    last = lax.broadcasted_iota(jnp.int32, (8, 128), 0) == 7

    def one_peer(peer, carry):
        move = moves_ref[0, 0, peer]
        moved = points_ref[jnp.maximum(move, 0)]
        moved = jnp.where(move >= 0, moved, jnp.zeros_like(moved))
        for o in range(3):
            block = points_ref[sends_ref[o, 0, peer]]
            out_ref[peer, 8 * o : 8 * o + 8] = jnp.where(last, moved[o : o + 1], block)
        return carry

    lax.fori_loop(0, out_ref.shape[0], one_peer, 0, unroll=8)


def local_kernel(
    pairs_ref, points_ref, mask_ref, totals_ref, feature_ref, sums_ref, turned_ref, weights_ref
):
    count = points_ref.shape[0]
    tiles = mask_ref.shape[0]
    sums_ref[...] = jnp.zeros_like(sums_ref)
    turn(lambda n: points_ref[n], turned_ref)

    def one_block(block, carry):
        feature_ref[block] = features(points_ref[block])
        return carry

    lax.fori_loop(0, count, one_block, 0, unroll=8)

    def words_of(slot, e):
        return jnp.concatenate([mask_ref[slot, pl.ds(j, 8, stride=0), :] for j in range(16)], axis=0)

    def store_other(slot, on_other):
        sums_ref[pairs_ref[1, slot]] += on_other

    tile_loop(
        tiles, 1, 4, lambda slot, e: pairs_ref[0, slot], lambda slot: pairs_ref[1, slot], None,
        words_of, turned_ref, points_ref, feature_ref, sums_ref, weights_ref, None, store_other,
    )

    def put(k, n, row):
        totals_ref[k, n : n + 16] = row

    block_terms(sums_ref, 0, points_ref, count, put)


def remote_kernel(parts, adds, earlier, local_ref, points_ref, feature_ref, mask_ref, *rest):
    sources, rest = rest[: len(parts)], rest[len(parts) :]
    add_refs, rest = rest[:adds], rest[adds:]
    earlier_refs, rest = rest[:earlier], rest[earlier:]
    totals_ref, rest = rest[0], rest[1:]
    back, rest = rest[: len(parts)], rest[len(parts) :]
    sums_ref, turned_ref, weights_ref, other_feature_ref, other_sums, blocks_ref = rest
    count = points_ref.shape[0]
    per_part = parts[0][3]
    slots = per_part * len(parts)
    starts = [group * first_of_group + first for group, _, first, _, first_of_group in parts]
    for n, (_, row, first, _, _) in enumerate(parts):
        for m in range(per_part):
            blocks_ref[n * per_part + m] = sources[n][first + m, row : row + 8]
    turn(lambda n: blocks_ref[n], turned_ref)
    sums_ref[...] = jnp.zeros_like(sums_ref)
    gap = starts[-1] - starts[0] - per_part

    def entry(slot):
        return slot + starts[0] + gap * (slot // per_part)

    def owned_of(slot, e):
        return local_ref[e, entry(slot)]

    def words_of(slot, e):
        tile = 2 * entry(slot) + e
        return jnp.concatenate([mask_ref[tile, pl.ds(j, 8, stride=0), :] for j in range(16)], axis=0)

    def store_other(slot, on_other):
        other_sums[slot] = on_other

    tile_loop(
        slots, 2, 2, owned_of, lambda slot: slot, lambda slot: blocks_ref[slot], words_of, turned_ref,
        points_ref, feature_ref, sums_ref, weights_ref, other_feature_ref, store_other,
    )
    for part in range(len(parts)):
        before = back[part].shape[0] - per_part
        if before:
            back[part][0:before] = earlier_refs[part][...]
        rows = back[part].reshape(back[part].shape[0] * 4, 128)

        def put_back(k, n, row):
            rows[pl.ds(4 * (before + n) + k, 16, stride=4), :] = row

        block_terms(other_sums, part * per_part, blocks_ref, per_part, put_back)

    def put(k, n, row):
        for add in add_refs:
            row = row + add[k, n : n + 16]
        totals_ref[k, n : n + 16] = row

    block_terms(sums_ref, 0, points_ref, count, put)


def update_kernel(
    sends_ref, moves_ref, totals_ref, returned_ref, fields_ref, velocity_ref, storage_ref,
    new_fields_ref, new_velocity_ref, moving_ref, down_ref, here_ref, up_ref, rows_ref,
):
    count = storage_ref.shape[0]
    peers = returned_ref.shape[0]
    sums_refs = (down_ref, here_ref, up_ref)
    for sums_ref in sums_refs:
        sums_ref[...] = jnp.zeros_like(sums_ref)

    def one_peer(peer, carry):
        for o, sums_ref in enumerate(sums_refs):
            sums_ref[sends_ref[o, 0, peer]] += returned_ref[peer, o]
        return carry

    lax.fori_loop(0, peers, one_peer, 0, unroll=8)
    flats = [sums_ref.reshape(count * 4, 128) for sums_ref in sums_refs]

    def total(k):
        down, here, up = (block_rows(flat, k, count, 4) for flat in flats)
        return totals_ref[k] + (down + here + up)

    rows = rows_ref.reshape(count * 8, 128)
    for k in range(3):
        speed = velocity_ref[k] + time_step * total(k)
        moved = block_rows(fields_ref, k, count, 4) + time_step * speed
        new_velocity_ref[k] = speed
        new_fields_ref[pl.ds(k, count, stride=4), :] = moved
        rows[pl.ds(k, count, stride=8), :] = moved
        rows[pl.ds(4 + k, count, stride=8), :] = speed
    stored = storage_ref[...]
    pressure = (
        block_rows(fields_ref, 3, count, 4)
        + time_step * total(3) / stored
    )
    new_fields_ref[pl.ds(3, count, stride=4), :] = pressure
    rows[pl.ds(3, count, stride=8), :] = pressure
    rows[pl.ds(7, count, stride=8), :] = stored

    def one_move(peer, carry):
        move = moves_ref[0, 0, peer]
        block = rows_ref[jnp.maximum(move, 0)]
        moving_ref[peer] = jnp.where(move >= 0, block, jnp.zeros_like(block))
        return carry

    lax.fori_loop(0, peers, one_move, 0, unroll=4)


def arrive_kernel(late_ref, early_ref, out_ref):
    peers = late_ref.shape[0]
    late = late_ref.reshape(peers * 8, 128)
    early = early_ref.reshape(peers * 24, 128)
    for k in range(7):
        out_ref[k] = block_rows(late, k, peers, 8)
    for k in range(3):
        out_ref[7 + k] = block_rows(early, 8 * k + 7, peers, 24)
    out_ref[10] = block_rows(late, 7, peers, 8)


def in_vmem():
    return pl.BlockSpec(memory_space=pltpu.VMEM)


def in_smem():
    return pl.BlockSpec(memory_space=pltpu.SMEM)


def params():
    return pltpu.CompilerParams(vmem_limit_bytes=vmem_bytes)


def cost(flops):
    return pl.CostEstimate(flops=flops, bytes_accessed=2 * 1024 * 1024, transcendentals=0)


def shape(*dims, dtype=f32):
    return jax.ShapeDtypeStruct(dims, dtype)


def anywhere():
    return pl.BlockSpec(memory_space=pl.ANY)


def remote_tiles(parts, local, points, feature, mask, sources, adds=(), earlier=()):
    count = points.shape[0]
    per_part = parts[0][3]
    slots = per_part * len(parts)
    before = earlier[0].shape[0] if earlier else 0
    return pl.pallas_call(
        functools.partial(remote_kernel, parts, len(adds), len(earlier)),
        out_shape=[shape(4, count, 128)] + [shape(before + per_part, 4, 128)] * len(parts),
        in_specs=[in_smem()] + [in_vmem()] * (3 + len(sources) + len(adds) + len(earlier)),
        out_specs=[in_vmem()] * (1 + len(parts)),
        scratch_shapes=[
            pltpu.VMEM((count, 16, 128), f32),
            pltpu.VMEM((slots // 16, 128, 128), f32),
            pltpu.VMEM((4, 4, 256, 256), bf16),
            pltpu.VMEM((4, 2, 48, 128), bf16),
            pltpu.VMEM((slots, 16, 128), f32),
            pltpu.VMEM((slots, 8, 128), f32),
        ],
        compiler_params=params(),
        cost_estimate=cost(slots * 10**8),
        name="remote_tiles",
    )(local, points, feature, mask, *sources, *adds, *earlier)


def local_tiles(pairs, points, mask):
    count = points.shape[0]
    return pl.pallas_call(
        local_kernel,
        out_shape=[shape(4, count, 128), shape(count, 48, 128, dtype=bf16)],
        in_specs=[in_smem(), in_vmem(), in_vmem()],
        out_specs=[in_vmem()] * 2,
        scratch_shapes=[
            pltpu.VMEM((count, 16, 128), f32),
            pltpu.VMEM((count // 16, 128, 128), f32),
            pltpu.VMEM((4, 4, 256, 256), bf16),
        ],
        compiler_params=params(),
        cost_estimate=cost(4 * 10**9),
        name="local_tiles",
    )(pairs, points, mask)


def per_device(
    positions,
    fields,
    storage,
    velocity,
    send_list,
    remote_local,
    remote_mask,
    local_pairs,
    local_mask,
    migrate_list,
):
    count = positions.shape[0]
    peers = send_list.shape[2]
    sends = send_list[0].transpose(0, 2, 1)
    moves = migrate_list.transpose(0, 2, 1)
    rows_first = positions.transpose(1, 0, 2)
    flat_fields = fields.reshape(count * 4, 128)
    outgoing, points = pl.pallas_call(
        pack_kernel,
        out_shape=[shape(peers, 24, 128), shape(count, 8, 128)],
        in_specs=[anywhere()] * 4,
        out_specs=[in_vmem()] * 2,
        scratch_shapes=[
            pltpu.SMEM(sends.shape, jnp.int32),
            pltpu.SMEM(moves.shape, jnp.int32),
            pltpu.VMEM(rows_first.shape, f32),
            pltpu.VMEM(flat_fields.shape, f32),
            pltpu.SemaphoreType.DMA((4,)),
        ],
        compiler_params=pltpu.CompilerParams(vmem_limit_bytes=60 * 1024 * 1024),
        name="pack",
    )(sends, moves, rows_first, flat_fields)
    spread = lax.all_to_all(outgoing, "bulk", split_axis=0, concat_axis=0, tiled=True)
    local_totals, feature = local_tiles(local_pairs[0].transpose(1, 0), points, local_mask[0])
    spread, feature = lax.optimization_barrier((spread, feature))
    local = remote_local[0].transpose(1, 0)
    mask = remote_mask[0].reshape(-1, remote_mask.shape[3], remote_mask.shape[4])
    tile_args = (local, points, feature, mask)
    down = from_behind(spread[:, 0:8], "region", -1)
    up = from_behind(spread[:, 16:24], "region", 1)
    half = peers // 2
    first_totals, first_back = remote_tiles(((1, 8, 0, half, peers),), *tile_args, [spread])
    far_totals, down_back, up_back = remote_tiles(
        ((0, 0, 0, peers, peers), (2, 0, 0, peers, peers)), *tile_args, [down, up]
    )
    down_back = from_behind(down_back, "region", 1)
    up_back = from_behind(up_back, "region", -1)
    totals, here_back = remote_tiles(
        ((1, 8, half, half, peers),), *tile_args, [spread],
        [local_totals, first_totals, far_totals], [first_back],
    )
    stacked = jnp.stack([down_back, here_back, up_back], axis=1)
    returned = lax.all_to_all(stacked, "bulk", split_axis=0, concat_axis=0, tiled=True)
    new_fields, new_velocity, moving = pl.pallas_call(
        update_kernel,
        out_shape=[shape(count * 4, 128), shape(3, count, 128), shape(peers, 8, 128)],
        in_specs=[in_smem()] * 2 + [in_vmem()] * 5,
        out_specs=[in_vmem()] * 3,
        scratch_shapes=[pltpu.VMEM((count, 4, 128), f32)] * 3 + [pltpu.VMEM((count, 8, 128), f32)],
        compiler_params=params(),
        name="update",
    )(sends, moves, totals, returned, flat_fields, velocity.transpose(1, 0, 2), storage)
    late = lax.all_to_all(moving, "bulk", split_axis=0, concat_axis=0, tiled=True)
    arrived = pl.pallas_call(
        arrive_kernel,
        out_shape=shape(11, peers, 128),
        in_specs=[in_vmem()] * 2,
        out_specs=in_vmem(),
        compiler_params=params(),
        name="arrive",
    )(late, spread)
    return (
        new_fields.reshape(count, 4, 128),
        new_velocity.transpose(1, 0, 2),
        arrived.transpose(1, 0, 2),
    )


def solution(mesh):
    spec = lambda rank: P(("region", "bulk"), *([None] * (rank - 1)))
    return jax.shard_map(
        per_device,
        mesh=mesh,
        in_specs=tuple(spec(rank) for rank in (3, 3, 2, 3, 4, 3, 5, 3, 4, 3)),
        out_specs=(spec(3), spec(3), spec(3)),
        check_vma=False,
    )
```

```python
import functools

import jax
import jax.numpy as jnp
from jax import lax
from jax.experimental import pallas as pl
from jax.experimental.pallas import tpu as pltpu
from jax.sharding import PartitionSpec as P

bond_stiff = 0.1
press_gain = 0.05
leak_gain = 0.5
time_step = 0.5
inv_horizon = 0.25
vmem_bytes = 40 * 1024 * 1024
f32 = jnp.float32
bf16 = jnp.bfloat16


def from_behind(shard, axis, by):
    peers = lax.axis_size(axis)
    return lax.ppermute(shard, axis, [(i, (i + by) % peers) for i in range(peers)])


def features(block):
    width = block.shape[1]
    x, p, u = block[0:3], block[3:4], block[4:7]
    one = jnp.ones((1, width), f32)
    rows = jnp.concatenate([x, p, p * x, one, u, one, jnp.zeros((4, width), f32)], axis=0)
    high = rows.astype(bf16)
    rest = rows - high.astype(f32)
    middle = rest.astype(bf16)
    low = (rest - middle.astype(f32)).astype(bf16)
    return jnp.concatenate([high, middle, low], axis=0)


def terms_of(sums, x, p, u):
    mean_gain = 0.5 * press_gain
    out = [
        bond_stiff * (sums[8 + k] - u[k] * sums[11])
        - mean_gain * (p * (sums[k] - x[k] * sums[7]) + (sums[4 + k] - x[k] * sums[3]))
        for k in range(3)
    ]
    out.append(leak_gain * (sums[3] - p * sums[7]))
    return out


def block_rows(ref, first, count, stride):
    return ref[pl.ds(first, count, stride=stride), :]


def turn(blocks, turned_ref):
    for g in range(turned_ref.shape[0]):
        group = jnp.concatenate([blocks(16 * g + n) for n in range(16)], axis=0)
        turned_ref[g] = 0.5 * jnp.transpose(group)


def bond_weights(others, owned, words, bits):
    apart = [others[k] - 0.5 * owned[k : k + 1] for k in range(3)]
    size = apart[0] * apart[0] + 1.0 + (apart[1] * apart[1] + apart[2] * apart[2])
    weight = pltpu.reciprocal(size, approx=True)
    intact = (words & bits) != 0
    high = weight.astype(bf16)
    low = (weight - high.astype(f32)).astype(bf16)
    none = jnp.zeros((128, 128), bf16)
    intact_high = jnp.where(intact, high, none)
    intact_low = jnp.where(intact, low, none)
    return intact_high, high, intact_low, low


def split_sums(product):
    product = product[0:16] + product[16:32] + product[32:48]
    intact, every = product[:, :128], product[:, 128:]
    return jnp.concatenate([every[0:8] - intact[0:8], intact[8:16]], axis=0)


def tile_sums(weights, owned_feature, other_feature):
    intact_high, high, intact_low, low = weights
    by_other = jnp.concatenate(
        [
            jnp.concatenate([intact_high, high], axis=1),
            jnp.concatenate([intact_low, low], axis=1),
        ],
        axis=0,
    )
    on_owned = jnp.dot(
        jnp.concatenate([other_feature, other_feature], axis=1),
        by_other,
        preferred_element_type=f32,
    )
    by_owned = jnp.concatenate(
        [
            jnp.concatenate([intact_high, intact_low], axis=1),
            jnp.concatenate([high, low], axis=1),
        ],
        axis=0,
    )
    on_other = lax.dot_general(
        jnp.concatenate([owned_feature, owned_feature], axis=1),
        by_owned,
        (((1,), (1,)), ((), ())),
        preferred_element_type=f32,
    )
    return split_sums(on_owned), split_sums(on_other)


def tile_loop(
    slots, touch, per_step, owned_of, other_of, other_block, words_of, turned_ref, points_ref,
    feature_ref, sums_ref, weights_ref, other_feature_ref, store_other,
):
    bits = jnp.left_shift(1, lax.broadcasted_iota(jnp.int32, (16, 8, 128), 1)).reshape(128, 128)
    steps = slots // per_step

    def weigh(step, half):
        for n in range(per_step):
            slot = step * per_step + n
            other = other_of(slot)
            if other_block is not None:
                other_feature_ref[half, n] = features(other_block(slot))
            turned = turned_ref[other // 16]
            lane = 8 * lax.rem(other, 16)
            others = [
                jnp.take_along_axis(turned, jnp.full((128, 128), lane + k, jnp.int32), axis=1)
                for k in range(3)
            ]
            for e in range(touch):
                owned = owned_of(slot, e)
                a, b, c, d = bond_weights(others, points_ref[owned], words_of(slot, e), bits)
                at = n * touch + e
                weights_ref[half, at, 0:128, 0:128] = a
                weights_ref[half, at, 0:128, 128:256] = b
                weights_ref[half, at, 128:256, 0:128] = c
                weights_ref[half, at, 128:256, 128:256] = d

    def add_up(step, half):
        for n in range(per_step):
            slot = step * per_step + n
            if other_block is not None:
                feature = other_feature_ref[half, n]
            else:
                feature = feature_ref[other_of(slot)]
            on_other = None
            for e in range(touch):
                owned = owned_of(slot, e)
                kept = weights_ref[half, n * touch + e]
                parts = (kept[:128, :128], kept[:128, 128:], kept[128:, :128], kept[128:, 128:])
                on_owned, more = tile_sums(parts, feature_ref[owned], feature)
                sums_ref[owned] += on_owned
                on_other = more if on_other is None else on_other + more
            store_other(slot, on_other)

    weigh(0, 0)

    def body(k, carry):
        for n in range(4):
            weigh(4 * k + n + 1, (n + 1) % 4)
            add_up(4 * k + n, n)
        return carry

    lax.fori_loop(0, steps // 4 - 1, body, 0)
    for n in range(4):
        if n < 3:
            weigh(steps - 3 + n, n + 1)
        add_up(steps - 4 + n, n)


def block_terms(sums_ref, first, blocks_ref, count, put):
    sums = sums_ref.reshape(sums_ref.shape[0] * 16, 128)
    rows = blocks_ref.reshape(blocks_ref.shape[0] * 8, 128)
    for n in range(0, count, 16):
        own = [block_rows(rows, 8 * (first + n) + r, 16, 8) for r in range(7)]
        terms = terms_of(
            [block_rows(sums, 16 * (first + n) + r, 16, 16) for r in range(12)],
            own[0:3],
            own[3],
            own[4:7],
        )
        for k, row in enumerate(terms):
            put(k, n, row)


def fetch(copies):
    for copy in copies:
        copy.start()
    for copy in copies:
        copy.wait()


def pack_kernel(
    sends_any, moves_any, positions_any, fields_any, out_any, points_any,
    sends_ref, moves_ref, positions_ref, fields_ref, out_ref, points_ref, sems,
):
    pairs = (
        (positions_any, positions_ref),
        (fields_any, fields_ref),
        (sends_any, sends_ref),
        (moves_any, moves_ref),
    )
    fetch([pltpu.make_async_copy(a, b, sems.at[n]) for n, (a, b) in enumerate(pairs)])
    count = positions_ref.shape[1]
    flat = points_ref.reshape(count * 8, 128)
    for k in range(3):
        flat[pl.ds(k, count, stride=8), :] = positions_ref[k]
        flat[pl.ds(4 + k, count, stride=8), :] = block_rows(fields_ref, k, count, 4)
    flat[pl.ds(3, count, stride=8), :] = block_rows(fields_ref, 3, count, 4)
    flat[pl.ds(7, count, stride=8), :] = jnp.zeros((count, 128), f32)
    away = [pltpu.make_async_copy(points_ref, points_any, sems.at[4])]
    away[0].start()
    last = lax.broadcasted_iota(jnp.int32, (8, 128), 0) == 7

    def one_peer(peer, carry):
        move = moves_ref[0, 0, peer]
        moved = points_ref[jnp.maximum(move, 0)]
        moved = jnp.where(move >= 0, moved, jnp.zeros_like(moved))
        for o in range(3):
            block = points_ref[sends_ref[o, 0, peer]]
            out_ref[peer, 8 * o : 8 * o + 8] = jnp.where(last, moved[o : o + 1], block)
        return carry

    peers = out_ref.shape[0]
    for n in range(4):
        low, high = n * peers // 4, (n + 1) * peers // 4
        lax.fori_loop(low, high, one_peer, 0, unroll=True)
        away.append(pltpu.make_async_copy(out_ref.at[low:high], out_any.at[low:high], sems.at[5 + n]))
        away[-1].start()
    for copy in away:
        copy.wait()


def local_kernel(
    pairs_ref, points_ref, mask_ref, totals_ref, feature_ref, sums_ref, turned_ref, weights_ref
):
    count = points_ref.shape[0]
    tiles = mask_ref.shape[0]
    sums_ref[...] = jnp.zeros_like(sums_ref)
    turn(lambda n: points_ref[n], turned_ref)

    def one_block(block, carry):
        feature_ref[block] = features(points_ref[block])
        return carry

    lax.fori_loop(0, count, one_block, 0, unroll=8)

    def words_of(slot, e):
        return jnp.concatenate([mask_ref[slot, pl.ds(j, 8, stride=0), :] for j in range(16)], axis=0)

    def store_other(slot, on_other):
        sums_ref[pairs_ref[1, slot]] += on_other

    tile_loop(
        tiles, 1, 4, lambda slot, e: pairs_ref[0, slot], lambda slot: pairs_ref[1, slot], None,
        words_of, turned_ref, points_ref, feature_ref, sums_ref, weights_ref, None, store_other,
    )

    def put(k, n, row):
        totals_ref[k, n : n + 16] = row

    block_terms(sums_ref, 0, points_ref, count, put)


def remote_kernel(parts, adds, earlier, local_ref, points_ref, feature_ref, mask_ref, *rest):
    sources, rest = rest[: len(parts)], rest[len(parts) :]
    add_refs, rest = rest[:adds], rest[adds:]
    earlier_refs, rest = rest[:earlier], rest[earlier:]
    totals_ref, rest = rest[0], rest[1:]
    back, rest = rest[: len(parts)], rest[len(parts) :]
    sums_ref, turned_ref, weights_ref, other_feature_ref, other_sums, blocks_ref = rest
    count = points_ref.shape[0]
    per_part = parts[0][3]
    slots = per_part * len(parts)
    starts = [group * first_of_group + first for group, _, first, _, first_of_group in parts]
    for n, (_, row, first, _, _) in enumerate(parts):
        for m in range(per_part):
            blocks_ref[n * per_part + m] = sources[n][first + m, row : row + 8]
    turn(lambda n: blocks_ref[n], turned_ref)
    sums_ref[...] = jnp.zeros_like(sums_ref)
    gap = starts[-1] - starts[0] - per_part

    def entry(slot):
        return slot + starts[0] + gap * (slot // per_part)

    def owned_of(slot, e):
        return local_ref[e, entry(slot)]

    def words_of(slot, e):
        tile = 2 * entry(slot) + e
        return jnp.concatenate([mask_ref[tile, pl.ds(j, 8, stride=0), :] for j in range(16)], axis=0)

    def store_other(slot, on_other):
        other_sums[slot] = on_other

    tile_loop(
        slots, 2, 2, owned_of, lambda slot: slot, lambda slot: blocks_ref[slot], words_of, turned_ref,
        points_ref, feature_ref, sums_ref, weights_ref, other_feature_ref, store_other,
    )
    for part in range(len(parts)):
        before = back[part].shape[0] - per_part
        if before:
            back[part][0:before] = earlier_refs[part][...]
        rows = back[part].reshape(back[part].shape[0] * 4, 128)

        def put_back(k, n, row):
            rows[pl.ds(4 * (before + n) + k, 16, stride=4), :] = row

        block_terms(other_sums, part * per_part, blocks_ref, per_part, put_back)

    def put(k, n, row):
        for add in add_refs:
            row = row + add[k, n : n + 16]
        totals_ref[k, n : n + 16] = row

    block_terms(sums_ref, 0, points_ref, count, put)


def update_kernel(
    sends_ref, moves_ref, totals_ref, returned_ref, fields_ref, velocity_ref, storage_ref,
    rows_ref, moving_ref, down_ref, here_ref, up_ref,
):
    count = storage_ref.shape[0]
    peers = returned_ref.shape[0]
    sums_refs = (down_ref, here_ref, up_ref)
    for sums_ref in sums_refs:
        sums_ref[...] = jnp.zeros_like(sums_ref)

    def one_peer(peer, carry):
        for o, sums_ref in enumerate(sums_refs):
            sums_ref[sends_ref[o, 0, peer]] += returned_ref[peer, o]
        return carry

    lax.fori_loop(0, peers, one_peer, 0, unroll=8)
    flats = [sums_ref.reshape(count * 4, 128) for sums_ref in sums_refs]

    def total(k):
        down, here, up = (block_rows(flat, k, count, 4) for flat in flats)
        return totals_ref[k] + (down + here + up)

    rows = rows_ref.reshape(count * 8, 128)
    for k in range(3):
        speed = velocity_ref[k] + time_step * total(k)
        moved = block_rows(fields_ref, k, count, 4) + time_step * speed
        rows[pl.ds(k, count, stride=8), :] = moved
        rows[pl.ds(4 + k, count, stride=8), :] = speed
    stored = storage_ref[...]
    pressure = (
        block_rows(fields_ref, 3, count, 4)
        + time_step * total(3) / stored
    )
    rows[pl.ds(3, count, stride=8), :] = pressure
    rows[pl.ds(7, count, stride=8), :] = stored

    def one_move(peer, carry):
        move = moves_ref[0, 0, peer]
        block = rows_ref[jnp.maximum(move, 0)]
        moving_ref[peer] = jnp.where(move >= 0, block, jnp.zeros_like(block))
        return carry

    lax.fori_loop(0, peers, one_move, 0, unroll=4)


def store_kernel(rows_ref, new_fields_ref, new_velocity_ref):
    count = rows_ref.shape[0]
    rows = rows_ref.reshape(count * 8, 128)
    for k in range(4):
        new_fields_ref[pl.ds(k, count, stride=4), :] = block_rows(rows, k, count, 8)
    for k in range(3):
        new_velocity_ref[k] = block_rows(rows, 4 + k, count, 8)


def arrive_kernel(late_ref, early_ref, out_ref):
    peers = late_ref.shape[0]
    late = late_ref.reshape(peers * 8, 128)
    early = early_ref.reshape(peers * 24, 128)
    for k in range(7):
        out_ref[k] = block_rows(late, k, peers, 8)
    for k in range(3):
        out_ref[7 + k] = block_rows(early, 8 * k + 7, peers, 24)
    out_ref[10] = block_rows(late, 7, peers, 8)


def in_vmem():
    return pl.BlockSpec(memory_space=pltpu.VMEM)


def in_smem():
    return pl.BlockSpec(memory_space=pltpu.SMEM)


def params():
    return pltpu.CompilerParams(vmem_limit_bytes=vmem_bytes)


def cost(flops):
    return pl.CostEstimate(flops=flops, bytes_accessed=2 * 1024 * 1024, transcendentals=0)


def shape(*dims, dtype=f32):
    return jax.ShapeDtypeStruct(dims, dtype)


def anywhere():
    return pl.BlockSpec(memory_space=pl.ANY)


def remote_tiles(parts, local, points, feature, mask, sources, adds=(), earlier=()):
    count = points.shape[0]
    per_part = parts[0][3]
    slots = per_part * len(parts)
    before = earlier[0].shape[0] if earlier else 0
    return pl.pallas_call(
        functools.partial(remote_kernel, parts, len(adds), len(earlier)),
        out_shape=[shape(4, count, 128)] + [shape(before + per_part, 4, 128)] * len(parts),
        in_specs=[in_smem()] + [in_vmem()] * (3 + len(sources) + len(adds) + len(earlier)),
        out_specs=[in_vmem()] * (1 + len(parts)),
        scratch_shapes=[
            pltpu.VMEM((count, 16, 128), f32),
            pltpu.VMEM((slots // 16, 128, 128), f32),
            pltpu.VMEM((4, 4, 256, 256), bf16),
            pltpu.VMEM((4, 2, 48, 128), bf16),
            pltpu.VMEM((slots, 16, 128), f32),
            pltpu.VMEM((slots, 8, 128), f32),
        ],
        compiler_params=params(),
        cost_estimate=cost(slots * 10**8),
        name="remote_tiles",
    )(local, points, feature, mask, *sources, *adds, *earlier)


def local_tiles(pairs, points, mask):
    count = points.shape[0]
    return pl.pallas_call(
        local_kernel,
        out_shape=[shape(4, count, 128), shape(count, 48, 128, dtype=bf16)],
        in_specs=[in_smem(), in_vmem(), in_vmem()],
        out_specs=[in_vmem()] * 2,
        scratch_shapes=[
            pltpu.VMEM((count, 16, 128), f32),
            pltpu.VMEM((count // 16, 128, 128), f32),
            pltpu.VMEM((4, 4, 256, 256), bf16),
        ],
        compiler_params=params(),
        cost_estimate=cost(4 * 10**9),
        name="local_tiles",
    )(pairs, points, mask)


def per_device(
    positions,
    fields,
    storage,
    velocity,
    send_list,
    remote_local,
    remote_mask,
    local_pairs,
    local_mask,
    migrate_list,
):
    count = positions.shape[0]
    peers = send_list.shape[2]
    sends = send_list[0].transpose(0, 2, 1)
    moves = migrate_list.transpose(0, 2, 1)
    rows_first = positions.transpose(1, 0, 2)
    flat_fields = fields.reshape(count * 4, 128)
    outgoing, points = pl.pallas_call(
        pack_kernel,
        out_shape=[shape(peers, 24, 128), shape(count, 8, 128)],
        in_specs=[anywhere()] * 4,
        out_specs=[anywhere()] * 2,
        scratch_shapes=[
            pltpu.SMEM(sends.shape, jnp.int32),
            pltpu.SMEM(moves.shape, jnp.int32),
            pltpu.VMEM(rows_first.shape, f32),
            pltpu.VMEM(flat_fields.shape, f32),
            pltpu.VMEM((peers, 24, 128), f32),
            pltpu.VMEM((count, 8, 128), f32),
            pltpu.SemaphoreType.DMA((9,)),
        ],
        compiler_params=pltpu.CompilerParams(vmem_limit_bytes=60 * 1024 * 1024),
        name="pack",
    )(sends, moves, rows_first, flat_fields)
    spread = lax.all_to_all(outgoing, "bulk", split_axis=0, concat_axis=0, tiled=True)
    local_totals, feature = local_tiles(local_pairs[0].transpose(1, 0), points, local_mask[0])
    spread, feature = lax.optimization_barrier((spread, feature))
    local = remote_local[0].transpose(1, 0)
    mask = remote_mask[0].reshape(-1, remote_mask.shape[3], remote_mask.shape[4])
    tile_args = (local, points, feature, mask)
    down = from_behind(spread[:, 0:8], "region", -1)
    up = from_behind(spread[:, 16:24], "region", 1)
    half = peers // 2
    first_totals, first_back = remote_tiles(((1, 8, 0, half, peers),), *tile_args, [spread])
    far_totals, down_back, up_back = remote_tiles(
        ((0, 0, 0, peers, peers), (2, 0, 0, peers, peers)), *tile_args, [down, up]
    )
    down_back = from_behind(down_back, "region", 1)
    up_back = from_behind(up_back, "region", -1)
    totals, here_back = remote_tiles(
        ((1, 8, half, half, peers),), *tile_args, [spread],
        [local_totals, first_totals, far_totals], [first_back],
    )
    stacked = jnp.stack([down_back, here_back, up_back], axis=1)
    returned = lax.all_to_all(stacked, "bulk", split_axis=0, concat_axis=0, tiled=True)
    rows, moving = pl.pallas_call(
        update_kernel,
        out_shape=[shape(count, 8, 128), shape(peers, 8, 128)],
        in_specs=[in_smem()] * 2 + [in_vmem()] * 5,
        out_specs=[in_vmem()] * 2,
        scratch_shapes=[pltpu.VMEM((count, 4, 128), f32)] * 3,
        compiler_params=params(),
        name="update",
    )(sends, moves, totals, returned, flat_fields, velocity.transpose(1, 0, 2), storage)
    late = lax.all_to_all(moving, "bulk", split_axis=0, concat_axis=0, tiled=True)
    new_fields, new_velocity = pl.pallas_call(
        store_kernel,
        out_shape=[shape(count * 4, 128), shape(3, count, 128)],
        in_specs=[in_vmem()],
        out_specs=[in_vmem()] * 2,
        compiler_params=params(),
        cost_estimate=cost(10**9),
        name="store",
    )(rows)
    arrived = pl.pallas_call(
        arrive_kernel,
        out_shape=shape(11, peers, 128),
        in_specs=[in_vmem()] * 2,
        out_specs=in_vmem(),
        compiler_params=params(),
        name="arrive",
    )(late, spread)
    return (
        new_fields.reshape(count, 4, 128),
        new_velocity.transpose(1, 0, 2),
        arrived.transpose(1, 0, 2),
    )


def solution(mesh):
    spec = lambda rank: P(("region", "bulk"), *([None] * (rank - 1)))
    return jax.shard_map(
        per_device,
        mesh=mesh,
        in_specs=tuple(spec(rank) for rank in (3, 3, 2, 3, 4, 3, 5, 3, 4, 3)),
        out_specs=(spec(3), spec(3), spec(3)),
        check_vma=False,
    )
```

```python
import functools

import jax
import jax.numpy as jnp
from jax import lax
from jax.experimental import pallas as pl
from jax.experimental.pallas import tpu as pltpu
from jax.sharding import PartitionSpec as P

bond_stiff = 0.1
press_gain = 0.05
leak_gain = 0.5
time_step = 0.5
inv_horizon = 0.25
vmem_bytes = 40 * 1024 * 1024
f32 = jnp.float32
bf16 = jnp.bfloat16


def from_behind(shard, axis, by):
    peers = lax.axis_size(axis)
    return lax.ppermute(shard, axis, [(i, (i + by) % peers) for i in range(peers)])


def features(block):
    width = block.shape[1]
    x, p, u = block[0:3], block[3:4], block[4:7]
    one = jnp.ones((1, width), f32)
    rows = jnp.concatenate([x, p, p * x, one, u, one, jnp.zeros((4, width), f32)], axis=0)
    high = rows.astype(bf16)
    rest = rows - high.astype(f32)
    middle = rest.astype(bf16)
    low = (rest - middle.astype(f32)).astype(bf16)
    return jnp.concatenate([high, middle, low], axis=0)


def terms_of(sums, x, p, u):
    mean_gain = 0.5 * press_gain
    out = [
        bond_stiff * (sums[8 + k] - u[k] * sums[11])
        - mean_gain * (p * (sums[k] - x[k] * sums[7]) + (sums[4 + k] - x[k] * sums[3]))
        for k in range(3)
    ]
    out.append(leak_gain * (sums[3] - p * sums[7]))
    return out


def block_rows(ref, first, count, stride):
    return ref[pl.ds(first, count, stride=stride), :]


def turn(blocks, turned_ref):
    for g in range(turned_ref.shape[0]):
        group = jnp.concatenate([blocks(16 * g + n) for n in range(16)], axis=0)
        turned_ref[g] = 0.5 * jnp.transpose(group)


def bond_weights(others, owned, words, bits):
    apart = [others[k] - 0.5 * owned[k : k + 1] for k in range(3)]
    size = apart[0] * apart[0] + 1.0 + (apart[1] * apart[1] + apart[2] * apart[2])
    weight = pltpu.reciprocal(size, approx=True)
    intact = (words & bits) != 0
    high = weight.astype(bf16)
    low = (weight - high.astype(f32)).astype(bf16)
    none = jnp.zeros((128, 128), bf16)
    intact_high = jnp.where(intact, high, none)
    intact_low = jnp.where(intact, low, none)
    return intact_high, high, intact_low, low


def split_sums(product):
    product = product[0:16] + product[16:32] + product[32:48]
    intact, every = product[:, :128], product[:, 128:]
    return jnp.concatenate([every[0:8] - intact[0:8], intact[8:16]], axis=0)


def tile_sums(weights, owned_feature, other_feature):
    intact_high, high, intact_low, low = weights
    by_other = jnp.concatenate(
        [
            jnp.concatenate([intact_high, high], axis=1),
            jnp.concatenate([intact_low, low], axis=1),
        ],
        axis=0,
    )
    on_owned = jnp.dot(
        jnp.concatenate([other_feature, other_feature], axis=1),
        by_other,
        preferred_element_type=f32,
    )
    by_owned = jnp.concatenate(
        [
            jnp.concatenate([intact_high, intact_low], axis=1),
            jnp.concatenate([high, low], axis=1),
        ],
        axis=0,
    )
    on_other = lax.dot_general(
        jnp.concatenate([owned_feature, owned_feature], axis=1),
        by_owned,
        (((1,), (1,)), ((), ())),
        preferred_element_type=f32,
    )
    return split_sums(on_owned), split_sums(on_other)


def tile_loop(
    slots, touch, per_step, owned_of, other_of, other_block, words_of, turned_ref, points_ref,
    feature_ref, sums_ref, weights_ref, other_feature_ref, store_other,
):
    bits = jnp.left_shift(1, lax.broadcasted_iota(jnp.int32, (16, 8, 128), 1)).reshape(128, 128)
    steps = slots // per_step

    def weigh(step, half):
        for n in range(per_step):
            slot = step * per_step + n
            other = other_of(slot)
            if other_block is not None:
                other_feature_ref[half, n] = features(other_block(slot))
            turned = turned_ref[other // 16]
            lane = 8 * lax.rem(other, 16)
            others = [
                jnp.take_along_axis(turned, jnp.full((128, 128), lane + k, jnp.int32), axis=1)
                for k in range(3)
            ]
            for e in range(touch):
                owned = owned_of(slot, e)
                a, b, c, d = bond_weights(others, points_ref[owned], words_of(slot, e), bits)
                at = n * touch + e
                weights_ref[half, at, 0:128, 0:128] = a
                weights_ref[half, at, 0:128, 128:256] = b
                weights_ref[half, at, 128:256, 0:128] = c
                weights_ref[half, at, 128:256, 128:256] = d

    def add_up(step, half):
        for n in range(per_step):
            slot = step * per_step + n
            if other_block is not None:
                feature = other_feature_ref[half, n]
            else:
                feature = feature_ref[other_of(slot)]
            on_other = None
            for e in range(touch):
                owned = owned_of(slot, e)
                kept = weights_ref[half, n * touch + e]
                parts = (kept[:128, :128], kept[:128, 128:], kept[128:, :128], kept[128:, 128:])
                on_owned, more = tile_sums(parts, feature_ref[owned], feature)
                sums_ref[owned] += on_owned
                on_other = more if on_other is None else on_other + more
            store_other(slot, on_other)

    weigh(0, 0)

    def body(k, carry):
        for n in range(4):
            weigh(4 * k + n + 1, (n + 1) % 4)
            add_up(4 * k + n, n)
        return carry

    lax.fori_loop(0, steps // 4 - 1, body, 0)
    for n in range(4):
        if n < 3:
            weigh(steps - 3 + n, n + 1)
        add_up(steps - 4 + n, n)


def block_terms(sums_ref, first, blocks_ref, count, put):
    sums = sums_ref.reshape(sums_ref.shape[0] * 16, 128)
    rows = blocks_ref.reshape(blocks_ref.shape[0] * 8, 128)
    for n in range(0, count, 16):
        own = [block_rows(rows, 8 * (first + n) + r, 16, 8) for r in range(7)]
        terms = terms_of(
            [block_rows(sums, 16 * (first + n) + r, 16, 16) for r in range(12)],
            own[0:3],
            own[3],
            own[4:7],
        )
        for k, row in enumerate(terms):
            put(k, n, row)


def fetch(copies):
    for copy in copies:
        copy.start()
    for copy in copies:
        copy.wait()


def pack_kernel(
    sends_any, moves_any, positions_any, fields_any, out_any, points_any,
    sends_ref, moves_ref, positions_ref, fields_ref, out_ref, points_ref, sems,
):
    pairs = (
        (positions_any, positions_ref),
        (fields_any, fields_ref),
        (sends_any, sends_ref),
        (moves_any, moves_ref),
    )
    fetch([pltpu.make_async_copy(a, b, sems.at[n]) for n, (a, b) in enumerate(pairs)])
    count = positions_ref.shape[1]
    flat = points_ref.reshape(count * 8, 128)
    for k in range(3):
        flat[pl.ds(k, count, stride=8), :] = positions_ref[k]
        flat[pl.ds(4 + k, count, stride=8), :] = block_rows(fields_ref, k, count, 4)
    flat[pl.ds(3, count, stride=8), :] = block_rows(fields_ref, 3, count, 4)
    flat[pl.ds(7, count, stride=8), :] = jnp.zeros((count, 128), f32)
    away = [pltpu.make_async_copy(points_ref, points_any, sems.at[4])]
    away[0].start()
    last = lax.broadcasted_iota(jnp.int32, (8, 128), 0) == 7

    def one_peer(peer, carry):
        move = moves_ref[0, 0, peer]
        moved = points_ref[jnp.maximum(move, 0)]
        moved = jnp.where(move >= 0, moved, jnp.zeros_like(moved))
        for o in range(3):
            block = points_ref[sends_ref[o, 0, peer]]
            out_ref[peer, 8 * o : 8 * o + 8] = jnp.where(last, moved[o : o + 1], block)
        return carry

    peers = out_ref.shape[0]
    for n in range(4):
        low, high = n * peers // 4, (n + 1) * peers // 4
        lax.fori_loop(low, high, one_peer, 0, unroll=True)
        away.append(pltpu.make_async_copy(out_ref.at[low:high], out_any.at[low:high], sems.at[5 + n]))
        away[-1].start()
    for copy in away:
        copy.wait()


def local_kernel(
    pairs_ref, points_ref, mask_ref, totals_ref, feature_ref, sums_ref, turned_ref, weights_ref
):
    count = points_ref.shape[0]
    tiles = mask_ref.shape[0]
    sums_ref[...] = jnp.zeros_like(sums_ref)
    turn(lambda n: points_ref[n], turned_ref)

    def one_block(block, carry):
        feature_ref[block] = features(points_ref[block])
        return carry

    lax.fori_loop(0, count, one_block, 0, unroll=8)

    def words_of(slot, e):
        return jnp.concatenate([mask_ref[slot, pl.ds(j, 8, stride=0), :] for j in range(16)], axis=0)

    def store_other(slot, on_other):
        sums_ref[pairs_ref[1, slot]] += on_other

    tile_loop(
        tiles, 1, 4, lambda slot, e: pairs_ref[0, slot], lambda slot: pairs_ref[1, slot], None,
        words_of, turned_ref, points_ref, feature_ref, sums_ref, weights_ref, None, store_other,
    )

    def put(k, n, row):
        totals_ref[k, n : n + 16] = row

    block_terms(sums_ref, 0, points_ref, count, put)


def remote_kernel(parts, adds, earlier, local_ref, points_ref, feature_ref, mask_ref, *rest):
    sources, rest = rest[: len(parts)], rest[len(parts) :]
    add_refs, rest = rest[:adds], rest[adds:]
    earlier_refs, rest = rest[:earlier], rest[earlier:]
    totals_ref, rest = rest[0], rest[1:]
    back, rest = rest[: len(parts)], rest[len(parts) :]
    sums_ref, turned_ref, weights_ref, other_feature_ref, other_sums, blocks_ref = rest
    count = points_ref.shape[0]
    per_part = parts[0][3]
    slots = per_part * len(parts)
    starts = [group * first_of_group + first for group, _, first, _, first_of_group in parts]
    for n, (_, row, first, _, _) in enumerate(parts):
        for m in range(per_part):
            blocks_ref[n * per_part + m] = sources[n][first + m, row : row + 8]
    turn(lambda n: blocks_ref[n], turned_ref)
    sums_ref[...] = jnp.zeros_like(sums_ref)
    gap = starts[-1] - starts[0] - per_part

    def entry(slot):
        return slot + starts[0] + gap * (slot // per_part)

    def owned_of(slot, e):
        return local_ref[e, entry(slot)]

    def words_of(slot, e):
        tile = 2 * entry(slot) + e
        return jnp.concatenate([mask_ref[tile, pl.ds(j, 8, stride=0), :] for j in range(16)], axis=0)

    def store_other(slot, on_other):
        other_sums[slot] = on_other

    tile_loop(
        slots, 2, 2, owned_of, lambda slot: slot, lambda slot: blocks_ref[slot], words_of, turned_ref,
        points_ref, feature_ref, sums_ref, weights_ref, other_feature_ref, store_other,
    )
    for part in range(len(parts)):
        before = back[part].shape[0] - per_part
        if before:
            back[part][0:before] = earlier_refs[part][...]
        rows = back[part].reshape(back[part].shape[0] * 4, 128)

        def put_back(k, n, row):
            rows[pl.ds(4 * (before + n) + k, 16, stride=4), :] = row

        block_terms(other_sums, part * per_part, blocks_ref, per_part, put_back)

    def put(k, n, row):
        for add in add_refs:
            row = row + add[k, n : n + 16]
        totals_ref[k, n : n + 16] = row

    block_terms(sums_ref, 0, points_ref, count, put)


def update_kernel(
    sends_ref, moves_ref, totals_ref, returned_ref, fields_ref, velocity_ref, storage_ref,
    rows_ref, moving_ref, down_ref, here_ref, up_ref,
):
    count = storage_ref.shape[0]
    peers = returned_ref.shape[0]
    sums_refs = (down_ref, here_ref, up_ref)
    for sums_ref in sums_refs:
        sums_ref[...] = jnp.zeros_like(sums_ref)

    def one_peer(peer, carry):
        for o, sums_ref in enumerate(sums_refs):
            sums_ref[sends_ref[o, 0, peer]] += returned_ref[peer, o]
        return carry

    lax.fori_loop(0, peers, one_peer, 0, unroll=8)
    flats = [sums_ref.reshape(count * 4, 128) for sums_ref in sums_refs]

    def total(k):
        down, here, up = (block_rows(flat, k, count, 4) for flat in flats)
        return totals_ref[k] + (down + here + up)

    rows = rows_ref.reshape(count * 8, 128)
    for k in range(3):
        speed = velocity_ref[k] + time_step * total(k)
        moved = block_rows(fields_ref, k, count, 4) + time_step * speed
        rows[pl.ds(k, count, stride=8), :] = moved
        rows[pl.ds(4 + k, count, stride=8), :] = speed
    stored = storage_ref[...]
    pressure = (
        block_rows(fields_ref, 3, count, 4)
        + time_step * total(3) / stored
    )
    rows[pl.ds(3, count, stride=8), :] = pressure
    rows[pl.ds(7, count, stride=8), :] = stored

    def one_move(peer, carry):
        move = moves_ref[0, 0, peer]
        block = rows_ref[jnp.maximum(move, 0)]
        moving_ref[peer] = jnp.where(move >= 0, block, jnp.zeros_like(block))
        return carry

    lax.fori_loop(0, peers, one_move, 0, unroll=4)


def store_kernel(rows_ref, new_fields_ref, new_velocity_ref):
    count = rows_ref.shape[0]
    rows = rows_ref.reshape(count * 8, 128)
    for k in range(4):
        new_fields_ref[pl.ds(k, count, stride=4), :] = block_rows(rows, k, count, 8)
    for k in range(3):
        new_velocity_ref[k] = block_rows(rows, 4 + k, count, 8)


def arrive_kernel(late_ref, early_ref, out_ref):
    peers = late_ref.shape[0]
    late = late_ref.reshape(peers * 8, 128)
    early = early_ref.reshape(peers * 24, 128)
    for k in range(7):
        out_ref[k] = block_rows(late, k, peers, 8)
    for k in range(3):
        out_ref[7 + k] = block_rows(early, 8 * k + 7, peers, 24)
    out_ref[10] = block_rows(late, 7, peers, 8)


def in_vmem():
    return pl.BlockSpec(memory_space=pltpu.VMEM)


def in_smem():
    return pl.BlockSpec(memory_space=pltpu.SMEM)


def params():
    return pltpu.CompilerParams(vmem_limit_bytes=vmem_bytes)


def cost(flops):
    return pl.CostEstimate(flops=flops, bytes_accessed=2 * 1024 * 1024, transcendentals=0)


def shape(*dims, dtype=f32):
    return jax.ShapeDtypeStruct(dims, dtype)


def anywhere():
    return pl.BlockSpec(memory_space=pl.ANY)


def remote_tiles(parts, local, points, feature, mask, sources, adds=(), earlier=()):
    count = points.shape[0]
    per_part = parts[0][3]
    slots = per_part * len(parts)
    before = earlier[0].shape[0] if earlier else 0
    return pl.pallas_call(
        functools.partial(remote_kernel, parts, len(adds), len(earlier)),
        out_shape=[shape(4, count, 128)] + [shape(before + per_part, 4, 128)] * len(parts),
        in_specs=[in_smem()] + [in_vmem()] * (3 + len(sources) + len(adds) + len(earlier)),
        out_specs=[in_vmem()] * (1 + len(parts)),
        scratch_shapes=[
            pltpu.VMEM((count, 16, 128), f32),
            pltpu.VMEM((slots // 16, 128, 128), f32),
            pltpu.VMEM((4, 4, 256, 256), bf16),
            pltpu.VMEM((4, 2, 48, 128), bf16),
            pltpu.VMEM((slots, 16, 128), f32),
            pltpu.VMEM((slots, 8, 128), f32),
        ],
        compiler_params=params(),
        cost_estimate=cost(slots * 10**8),
        name="remote_tiles",
    )(local, points, feature, mask, *sources, *adds, *earlier)


def local_tiles(pairs, points, mask):
    count = points.shape[0]
    return pl.pallas_call(
        local_kernel,
        out_shape=[shape(4, count, 128), shape(count, 48, 128, dtype=bf16)],
        in_specs=[in_smem(), in_vmem(), in_vmem()],
        out_specs=[in_vmem()] * 2,
        scratch_shapes=[
            pltpu.VMEM((count, 16, 128), f32),
            pltpu.VMEM((count // 16, 128, 128), f32),
            pltpu.VMEM((4, 4, 256, 256), bf16),
        ],
        compiler_params=params(),
        cost_estimate=cost(4 * 10**9),
        name="local_tiles",
    )(pairs, points, mask)


def per_device(
    positions,
    fields,
    storage,
    velocity,
    send_list,
    remote_local,
    remote_mask,
    local_pairs,
    local_mask,
    migrate_list,
):
    count = positions.shape[0]
    peers = send_list.shape[2]
    sends = send_list[0].transpose(0, 2, 1)
    moves = migrate_list.transpose(0, 2, 1)
    rows_first = positions.transpose(1, 0, 2)
    flat_fields = fields.reshape(count * 4, 128)
    outgoing, points = pl.pallas_call(
        pack_kernel,
        out_shape=[shape(peers, 24, 128), shape(count, 8, 128)],
        in_specs=[anywhere()] * 4,
        out_specs=[anywhere()] * 2,
        scratch_shapes=[
            pltpu.SMEM(sends.shape, jnp.int32),
            pltpu.SMEM(moves.shape, jnp.int32),
            pltpu.VMEM(rows_first.shape, f32),
            pltpu.VMEM(flat_fields.shape, f32),
            pltpu.VMEM((peers, 24, 128), f32),
            pltpu.VMEM((count, 8, 128), f32),
            pltpu.SemaphoreType.DMA((9,)),
        ],
        compiler_params=pltpu.CompilerParams(vmem_limit_bytes=60 * 1024 * 1024),
        name="pack",
    )(sends, moves, rows_first, flat_fields)
    spread = lax.all_to_all(outgoing, "bulk", split_axis=0, concat_axis=0, tiled=True)
    local_totals, feature = local_tiles(local_pairs[0].transpose(1, 0), points, local_mask[0])
    spread, feature = lax.optimization_barrier((spread, feature))
    local = remote_local[0].transpose(1, 0)
    mask = remote_mask[0].reshape(-1, remote_mask.shape[3], remote_mask.shape[4])
    tile_args = (local, points, feature, mask)
    up = from_behind(spread[:, 16:24], "region", 1)
    down = from_behind(spread[:, 0:8], "region", -1)
    half = peers // 2
    first_totals, first_back = remote_tiles(((1, 8, 0, half, peers),), *tile_args, [spread])
    far_totals, up_back, down_back = remote_tiles(
        ((2, 0, 0, peers, peers), (0, 0, 0, peers, peers)), *tile_args, [up, down]
    )
    down_back = from_behind(down_back, "region", 1)
    up_back = from_behind(up_back, "region", -1)
    totals, here_back = remote_tiles(
        ((1, 8, half, half, peers),), *tile_args, [spread],
        [local_totals, first_totals, far_totals], [first_back],
    )
    stacked = jnp.stack([down_back, here_back, up_back], axis=1)
    returned = lax.all_to_all(stacked, "bulk", split_axis=0, concat_axis=0, tiled=True)
    rows, moving = pl.pallas_call(
        update_kernel,
        out_shape=[shape(count, 8, 128), shape(peers, 8, 128)],
        in_specs=[in_smem()] * 2 + [in_vmem()] * 5,
        out_specs=[in_vmem()] * 2,
        scratch_shapes=[pltpu.VMEM((count, 4, 128), f32)] * 3,
        compiler_params=params(),
        name="update",
    )(sends, moves, totals, returned, flat_fields, velocity.transpose(1, 0, 2), storage)
    late = lax.all_to_all(moving, "bulk", split_axis=0, concat_axis=0, tiled=True)
    new_fields, new_velocity = pl.pallas_call(
        store_kernel,
        out_shape=[shape(count * 4, 128), shape(3, count, 128)],
        in_specs=[in_vmem()],
        out_specs=[in_vmem()] * 2,
        compiler_params=params(),
        cost_estimate=cost(10**9),
        name="store",
    )(rows)
    arrived = pl.pallas_call(
        arrive_kernel,
        out_shape=shape(11, peers, 128),
        in_specs=[in_vmem()] * 2,
        out_specs=in_vmem(),
        compiler_params=params(),
        name="arrive",
    )(late, spread)
    return (
        new_fields.reshape(count, 4, 128),
        new_velocity.transpose(1, 0, 2),
        arrived.transpose(1, 0, 2),
    )


def solution(mesh):
    spec = lambda rank: P(("region", "bulk"), *([None] * (rank - 1)))
    return jax.shard_map(
        per_device,
        mesh=mesh,
        in_specs=tuple(spec(rank) for rank in (3, 3, 2, 3, 4, 3, 5, 3, 4, 3)),
        out_specs=(spec(3), spec(3), spec(3)),
        check_vma=False,
    )
```

```python
import functools

import jax
import jax.numpy as jnp
from jax import lax
from jax.experimental import pallas as pl
from jax.experimental.pallas import tpu as pltpu
from jax.sharding import PartitionSpec as P

bond_stiff = 0.1
press_gain = 0.05
leak_gain = 0.5
time_step = 0.5
inv_horizon = 0.25
vmem_bytes = 40 * 1024 * 1024
f32 = jnp.float32
bf16 = jnp.bfloat16


def from_behind(shard, axis, by):
    peers = lax.axis_size(axis)
    return lax.ppermute(shard, axis, [(i, (i + by) % peers) for i in range(peers)])


def features(block):
    width = block.shape[1]
    x, p, u = block[0:3], block[3:4], block[4:7]
    one = jnp.ones((1, width), f32)
    rows = jnp.concatenate([x, p, p * x, one, u, one, jnp.zeros((4, width), f32)], axis=0)
    high = rows.astype(bf16)
    rest = rows - high.astype(f32)
    middle = rest.astype(bf16)
    low = (rest - middle.astype(f32)).astype(bf16)
    return jnp.concatenate([high, middle, low], axis=0)


def terms_of(sums, x, p, u):
    mean_gain = 0.5 * press_gain
    out = [
        bond_stiff * (sums[8 + k] - u[k] * sums[11])
        - mean_gain * (p * (sums[k] - x[k] * sums[7]) + (sums[4 + k] - x[k] * sums[3]))
        for k in range(3)
    ]
    out.append(leak_gain * (sums[3] - p * sums[7]))
    return out


def block_rows(ref, first, count, stride):
    return ref[pl.ds(first, count, stride=stride), :]


def turn(blocks, turned_ref):
    for g in range(turned_ref.shape[0]):
        group = jnp.concatenate([blocks(16 * g + n) for n in range(16)], axis=0)
        turned_ref[g] = 0.5 * jnp.transpose(group)


def bond_weights(others, owned, words, bits):
    apart = [others[k] - 0.5 * owned[k : k + 1] for k in range(3)]
    size = apart[0] * apart[0] + 1.0 + (apart[1] * apart[1] + apart[2] * apart[2])
    weight = pltpu.reciprocal(size, approx=True)
    intact = (words & bits) != 0
    high = weight.astype(bf16)
    low = (weight - high.astype(f32)).astype(bf16)
    none = jnp.zeros((128, 128), bf16)
    intact_high = jnp.where(intact, high, none)
    intact_low = jnp.where(intact, low, none)
    return intact_high, high, intact_low, low


def split_sums(product):
    product = product[0:16] + product[16:32] + product[32:48]
    intact, every = product[:, :128], product[:, 128:]
    return jnp.concatenate([every[0:8] - intact[0:8], intact[8:16]], axis=0)


def tile_sums(weights, owned_feature, other_feature):
    intact_high, high, intact_low, low = weights
    by_other = jnp.concatenate(
        [
            jnp.concatenate([intact_high, high], axis=1),
            jnp.concatenate([intact_low, low], axis=1),
        ],
        axis=0,
    )
    on_owned = jnp.dot(
        jnp.concatenate([other_feature, other_feature], axis=1),
        by_other,
        preferred_element_type=f32,
    )
    by_owned = jnp.concatenate(
        [
            jnp.concatenate([intact_high, intact_low], axis=1),
            jnp.concatenate([high, low], axis=1),
        ],
        axis=0,
    )
    on_other = lax.dot_general(
        jnp.concatenate([owned_feature, owned_feature], axis=1),
        by_owned,
        (((1,), (1,)), ((), ())),
        preferred_element_type=f32,
    )
    return split_sums(on_owned), split_sums(on_other)


def tile_loop(
    slots, touch, per_step, owned_of, other_of, other_block, words_of, turned_ref, points_ref,
    feature_ref, sums_ref, weights_ref, other_feature_ref, store_other,
):
    bits = jnp.left_shift(1, lax.broadcasted_iota(jnp.int32, (16, 8, 128), 1)).reshape(128, 128)
    steps = slots // per_step

    def weigh(step, half):
        for n in range(per_step):
            slot = step * per_step + n
            other = other_of(slot)
            if other_block is not None:
                other_feature_ref[half, n] = features(other_block(slot))
            turned = turned_ref[other // 16]
            lane = 8 * lax.rem(other, 16)
            others = [
                jnp.take_along_axis(turned, jnp.full((128, 128), lane + k, jnp.int32), axis=1)
                for k in range(3)
            ]
            for e in range(touch):
                owned = owned_of(slot, e)
                a, b, c, d = bond_weights(others, points_ref[owned], words_of(slot, e), bits)
                at = n * touch + e
                weights_ref[half, at, 0:128, 0:128] = a
                weights_ref[half, at, 0:128, 128:256] = b
                weights_ref[half, at, 128:256, 0:128] = c
                weights_ref[half, at, 128:256, 128:256] = d

    def add_up(step, half):
        for n in range(per_step):
            slot = step * per_step + n
            if other_block is not None:
                feature = other_feature_ref[half, n]
            else:
                feature = feature_ref[other_of(slot)]
            on_other = None
            for e in range(touch):
                owned = owned_of(slot, e)
                kept = weights_ref[half, n * touch + e]
                parts = (kept[:128, :128], kept[:128, 128:], kept[128:, :128], kept[128:, 128:])
                on_owned, more = tile_sums(parts, feature_ref[owned], feature)
                sums_ref[owned] += on_owned
                on_other = more if on_other is None else on_other + more
            store_other(slot, on_other)

    weigh(0, 0)

    def body(k, carry):
        for n in range(4):
            weigh(4 * k + n + 1, (n + 1) % 4)
            add_up(4 * k + n, n)
        return carry

    lax.fori_loop(0, steps // 4 - 1, body, 0)
    for n in range(4):
        if n < 3:
            weigh(steps - 3 + n, n + 1)
        add_up(steps - 4 + n, n)


def block_terms(sums_ref, first, blocks_ref, count, put):
    sums = sums_ref.reshape(sums_ref.shape[0] * 16, 128)
    rows = blocks_ref.reshape(blocks_ref.shape[0] * 8, 128)
    for n in range(0, count, 16):
        own = [block_rows(rows, 8 * (first + n) + r, 16, 8) for r in range(7)]
        terms = terms_of(
            [block_rows(sums, 16 * (first + n) + r, 16, 16) for r in range(12)],
            own[0:3],
            own[3],
            own[4:7],
        )
        for k, row in enumerate(terms):
            put(k, n, row)


def fetch(copies):
    for copy in copies:
        copy.start()
    for copy in copies:
        copy.wait()


def pack_kernel(
    sends_any, moves_any, positions_any, fields_any, out_any, points_any,
    sends_ref, moves_ref, positions_ref, fields_ref, out_ref, points_ref, sems,
):
    pairs = (
        (positions_any, positions_ref),
        (fields_any, fields_ref),
        (sends_any, sends_ref),
        (moves_any, moves_ref),
    )
    fetch([pltpu.make_async_copy(a, b, sems.at[n]) for n, (a, b) in enumerate(pairs)])
    count = positions_ref.shape[1]
    flat = points_ref.reshape(count * 8, 128)
    for k in range(3):
        flat[pl.ds(k, count, stride=8), :] = positions_ref[k]
        flat[pl.ds(4 + k, count, stride=8), :] = block_rows(fields_ref, k, count, 4)
    flat[pl.ds(3, count, stride=8), :] = block_rows(fields_ref, 3, count, 4)
    flat[pl.ds(7, count, stride=8), :] = jnp.zeros((count, 128), f32)
    away = [pltpu.make_async_copy(points_ref, points_any, sems.at[4])]
    away[0].start()
    last = lax.broadcasted_iota(jnp.int32, (8, 128), 0) == 7

    def one_peer(peer, carry):
        move = moves_ref[0, 0, peer]
        moved = points_ref[jnp.maximum(move, 0)]
        moved = jnp.where(move >= 0, moved, jnp.zeros_like(moved))
        for o in range(3):
            block = points_ref[sends_ref[o, 0, peer]]
            out_ref[peer, 8 * o : 8 * o + 8] = jnp.where(last, moved[o : o + 1], block)
        return carry

    peers = out_ref.shape[0]
    for n in range(4):
        low, high = n * peers // 4, (n + 1) * peers // 4
        lax.fori_loop(low, high, one_peer, 0, unroll=True)
        away.append(pltpu.make_async_copy(out_ref.at[low:high], out_any.at[low:high], sems.at[5 + n]))
        away[-1].start()
    for copy in away:
        copy.wait()


def local_kernel(
    pairs_ref, points_ref, mask_ref, totals_ref, feature_ref, sums_ref, turned_ref, weights_ref
):
    count = points_ref.shape[0]
    tiles = mask_ref.shape[0]
    sums_ref[...] = jnp.zeros_like(sums_ref)
    turn(lambda n: points_ref[n], turned_ref)

    def one_block(block, carry):
        feature_ref[block] = features(points_ref[block])
        return carry

    lax.fori_loop(0, count, one_block, 0, unroll=8)

    def words_of(slot, e):
        return jnp.concatenate([mask_ref[slot, pl.ds(j, 8, stride=0), :] for j in range(16)], axis=0)

    def store_other(slot, on_other):
        sums_ref[pairs_ref[1, slot]] += on_other

    tile_loop(
        tiles, 1, 4, lambda slot, e: pairs_ref[0, slot], lambda slot: pairs_ref[1, slot], None,
        words_of, turned_ref, points_ref, feature_ref, sums_ref, weights_ref, None, store_other,
    )

    def put(k, n, row):
        totals_ref[k, n : n + 16] = row

    block_terms(sums_ref, 0, points_ref, count, put)


def remote_kernel(parts, adds, earlier, local_ref, points_ref, feature_ref, mask_ref, *rest):
    sources, rest = rest[: len(parts)], rest[len(parts) :]
    add_refs, rest = rest[:adds], rest[adds:]
    earlier_refs, rest = rest[:earlier], rest[earlier:]
    totals_ref, rest = rest[0], rest[1:]
    back, rest = rest[: len(parts)], rest[len(parts) :]
    sums_ref, turned_ref, weights_ref, other_feature_ref, other_sums, blocks_ref = rest
    count = points_ref.shape[0]
    per_part = parts[0][3]
    slots = per_part * len(parts)
    starts = [group * first_of_group + first for group, _, first, _, first_of_group in parts]
    for n, (_, row, first, _, _) in enumerate(parts):
        for m in range(per_part):
            blocks_ref[n * per_part + m] = sources[n][first + m, row : row + 8]
    turn(lambda n: blocks_ref[n], turned_ref)
    sums_ref[...] = jnp.zeros_like(sums_ref)
    gap = starts[-1] - starts[0] - per_part

    def entry(slot):
        return slot + starts[0] + gap * (slot // per_part)

    def owned_of(slot, e):
        return local_ref[e, entry(slot)]

    def words_of(slot, e):
        tile = 2 * entry(slot) + e
        return jnp.concatenate([mask_ref[tile, pl.ds(j, 8, stride=0), :] for j in range(16)], axis=0)

    def store_other(slot, on_other):
        other_sums[slot] = on_other

    tile_loop(
        slots, 2, 2, owned_of, lambda slot: slot, lambda slot: blocks_ref[slot], words_of, turned_ref,
        points_ref, feature_ref, sums_ref, weights_ref, other_feature_ref, store_other,
    )
    for part in range(len(parts)):
        before = back[part].shape[0] - per_part
        if before:
            back[part][0:before] = earlier_refs[part][...]
        rows = back[part].reshape(back[part].shape[0] * 4, 128)

        def put_back(k, n, row):
            rows[pl.ds(4 * (before + n) + k, 16, stride=4), :] = row

        block_terms(other_sums, part * per_part, blocks_ref, per_part, put_back)

    def put(k, n, row):
        for add in add_refs:
            row = row + add[k, n : n + 16]
        totals_ref[k, n : n + 16] = row

    block_terms(sums_ref, 0, points_ref, count, put)


def update_kernel(
    sends_ref, moves_ref, totals_ref, returned_ref, fields_ref, velocity_ref, storage_ref,
    new_fields_ref, new_velocity_ref, moving_ref, down_ref, here_ref, up_ref, rows_ref,
):
    count = storage_ref.shape[0]
    peers = returned_ref.shape[0]
    sums_refs = (down_ref, here_ref, up_ref)
    for sums_ref in sums_refs:
        sums_ref[...] = jnp.zeros_like(sums_ref)

    def one_peer(peer, carry):
        for o, sums_ref in enumerate(sums_refs):
            sums_ref[sends_ref[o, 0, peer]] += returned_ref[peer, o]
        return carry

    lax.fori_loop(0, peers, one_peer, 0, unroll=True)
    flats = [sums_ref.reshape(count * 4, 128) for sums_ref in sums_refs]

    def total(k):
        down, here, up = (block_rows(flat, k, count, 4) for flat in flats)
        return totals_ref[k] + (down + here + up)

    rows = rows_ref.reshape(count * 8, 128)
    for k in range(3):
        speed = velocity_ref[k] + time_step * total(k)
        moved = block_rows(fields_ref, k, count, 4) + time_step * speed
        new_velocity_ref[k] = speed
        new_fields_ref[pl.ds(k, count, stride=4), :] = moved
        rows[pl.ds(k, count, stride=8), :] = moved
        rows[pl.ds(4 + k, count, stride=8), :] = speed
    stored = storage_ref[...]
    pressure = (
        block_rows(fields_ref, 3, count, 4)
        + time_step * total(3) / stored
    )
    new_fields_ref[pl.ds(3, count, stride=4), :] = pressure
    rows[pl.ds(3, count, stride=8), :] = pressure
    rows[pl.ds(7, count, stride=8), :] = stored

    def one_move(peer, carry):
        move = moves_ref[0, 0, peer]
        block = rows_ref[jnp.maximum(move, 0)]
        moving_ref[peer] = jnp.where(move >= 0, block, jnp.zeros_like(block))
        return carry

    lax.fori_loop(0, peers, one_move, 0, unroll=True)


def arrive_kernel(late_ref, early_ref, out_ref):
    peers = late_ref.shape[0]
    late = late_ref.reshape(peers * 8, 128)
    early = early_ref.reshape(peers * 24, 128)
    for k in range(7):
        out_ref[k] = block_rows(late, k, peers, 8)
    for k in range(3):
        out_ref[7 + k] = block_rows(early, 8 * k + 7, peers, 24)
    out_ref[10] = block_rows(late, 7, peers, 8)


def in_vmem():
    return pl.BlockSpec(memory_space=pltpu.VMEM)


def in_smem():
    return pl.BlockSpec(memory_space=pltpu.SMEM)


def params():
    return pltpu.CompilerParams(vmem_limit_bytes=vmem_bytes)


def cost(flops):
    return pl.CostEstimate(flops=flops, bytes_accessed=2 * 1024 * 1024, transcendentals=0)


def shape(*dims, dtype=f32):
    return jax.ShapeDtypeStruct(dims, dtype)


def anywhere():
    return pl.BlockSpec(memory_space=pl.ANY)


def remote_tiles(parts, local, points, feature, mask, sources, adds=(), earlier=()):
    count = points.shape[0]
    per_part = parts[0][3]
    slots = per_part * len(parts)
    before = earlier[0].shape[0] if earlier else 0
    return pl.pallas_call(
        functools.partial(remote_kernel, parts, len(adds), len(earlier)),
        out_shape=[shape(4, count, 128)] + [shape(before + per_part, 4, 128)] * len(parts),
        in_specs=[in_smem()] + [in_vmem()] * (3 + len(sources) + len(adds) + len(earlier)),
        out_specs=[in_vmem()] * (1 + len(parts)),
        scratch_shapes=[
            pltpu.VMEM((count, 16, 128), f32),
            pltpu.VMEM((slots // 16, 128, 128), f32),
            pltpu.VMEM((4, 4, 256, 256), bf16),
            pltpu.VMEM((4, 2, 48, 128), bf16),
            pltpu.VMEM((slots, 16, 128), f32),
            pltpu.VMEM((slots, 8, 128), f32),
        ],
        compiler_params=params(),
        cost_estimate=cost(slots * 10**8),
        name="remote_tiles",
    )(local, points, feature, mask, *sources, *adds, *earlier)


def local_tiles(pairs, points, mask):
    count = points.shape[0]
    return pl.pallas_call(
        local_kernel,
        out_shape=[shape(4, count, 128), shape(count, 48, 128, dtype=bf16)],
        in_specs=[in_smem(), in_vmem(), in_vmem()],
        out_specs=[in_vmem()] * 2,
        scratch_shapes=[
            pltpu.VMEM((count, 16, 128), f32),
            pltpu.VMEM((count // 16, 128, 128), f32),
            pltpu.VMEM((4, 4, 256, 256), bf16),
        ],
        compiler_params=params(),
        cost_estimate=cost(4 * 10**9),
        name="local_tiles",
    )(pairs, points, mask)


def per_device(
    positions,
    fields,
    storage,
    velocity,
    send_list,
    remote_local,
    remote_mask,
    local_pairs,
    local_mask,
    migrate_list,
):
    count = positions.shape[0]
    peers = send_list.shape[2]
    sends = send_list[0].transpose(0, 2, 1)
    moves = migrate_list.transpose(0, 2, 1)
    rows_first = positions.transpose(1, 0, 2)
    flat_fields = fields.reshape(count * 4, 128)
    outgoing, points = pl.pallas_call(
        pack_kernel,
        out_shape=[shape(peers, 24, 128), shape(count, 8, 128)],
        in_specs=[anywhere()] * 4,
        out_specs=[anywhere()] * 2,
        scratch_shapes=[
            pltpu.SMEM(sends.shape, jnp.int32),
            pltpu.SMEM(moves.shape, jnp.int32),
            pltpu.VMEM(rows_first.shape, f32),
            pltpu.VMEM(flat_fields.shape, f32),
            pltpu.VMEM((peers, 24, 128), f32),
            pltpu.VMEM((count, 8, 128), f32),
            pltpu.SemaphoreType.DMA((9,)),
        ],
        compiler_params=pltpu.CompilerParams(vmem_limit_bytes=60 * 1024 * 1024),
        name="pack",
    )(sends, moves, rows_first, flat_fields)
    spread = lax.all_to_all(outgoing, "bulk", split_axis=0, concat_axis=0, tiled=True)
    local_totals, feature = local_tiles(local_pairs[0].transpose(1, 0), points, local_mask[0])
    spread, feature = lax.optimization_barrier((spread, feature))
    local = remote_local[0].transpose(1, 0)
    mask = remote_mask[0].reshape(-1, remote_mask.shape[3], remote_mask.shape[4])
    tile_args = (local, points, feature, mask)
    up = from_behind(spread[:, 16:24], "region", 1)
    down = from_behind(spread[:, 0:8], "region", -1)
    half = peers // 2
    first_totals, first_back = remote_tiles(((1, 8, 0, half, peers),), *tile_args, [spread])
    far_totals, up_back, down_back = remote_tiles(
        ((2, 0, 0, peers, peers), (0, 0, 0, peers, peers)), *tile_args, [up, down]
    )
    down_back = from_behind(down_back, "region", 1)
    up_back = from_behind(up_back, "region", -1)
    totals, here_back = remote_tiles(
        ((1, 8, half, half, peers),), *tile_args, [spread],
        [local_totals, first_totals, far_totals], [first_back],
    )
    stacked = jnp.stack([down_back, here_back, up_back], axis=1)
    returned = lax.all_to_all(stacked, "bulk", split_axis=0, concat_axis=0, tiled=True)
    new_fields, new_velocity, moving = pl.pallas_call(
        update_kernel,
        out_shape=[shape(count * 4, 128), shape(3, count, 128), shape(peers, 8, 128)],
        in_specs=[in_smem()] * 2 + [in_vmem()] * 5,
        out_specs=[in_vmem()] * 3,
        scratch_shapes=[pltpu.VMEM((count, 4, 128), f32)] * 3 + [pltpu.VMEM((count, 8, 128), f32)],
        compiler_params=params(),
        name="update",
    )(sends, moves, totals, returned, flat_fields, velocity.transpose(1, 0, 2), storage)
    late = lax.all_to_all(moving, "bulk", split_axis=0, concat_axis=0, tiled=True)
    arrived = pl.pallas_call(
        arrive_kernel,
        out_shape=shape(11, peers, 128),
        in_specs=[in_vmem()] * 2,
        out_specs=in_vmem(),
        compiler_params=params(),
        name="arrive",
    )(late, spread)
    return (
        new_fields.reshape(count, 4, 128),
        new_velocity.transpose(1, 0, 2),
        arrived.transpose(1, 0, 2),
    )


def solution(mesh):
    spec = lambda rank: P(("region", "bulk"), *([None] * (rank - 1)))
    return jax.shard_map(
        per_device,
        mesh=mesh,
        in_specs=tuple(spec(rank) for rank in (3, 3, 2, 3, 4, 3, 5, 3, 4, 3)),
        out_specs=(spec(3), spec(3), spec(3)),
        check_vma=False,
    )
```

```python
import functools

import jax
import jax.numpy as jnp
from jax import lax
from jax.experimental import pallas as pl
from jax.experimental.pallas import tpu as pltpu
from jax.sharding import PartitionSpec as P

bond_stiff = 0.1
press_gain = 0.05
leak_gain = 0.5
time_step = 0.5
inv_horizon = 0.25
vmem_bytes = 40 * 1024 * 1024
f32 = jnp.float32
bf16 = jnp.bfloat16


def from_behind(shard, axis, by):
    peers = lax.axis_size(axis)
    return lax.ppermute(shard, axis, [(i, (i + by) % peers) for i in range(peers)])


def features(block):
    width = block.shape[1]
    x, p, u = block[0:3], block[3:4], block[4:7]
    one = jnp.ones((1, width), f32)
    rows = jnp.concatenate([x, p, p * x, one, u, one, jnp.zeros((4, width), f32)], axis=0)
    high = rows.astype(bf16)
    rest = rows - high.astype(f32)
    middle = rest.astype(bf16)
    low = (rest - middle.astype(f32)).astype(bf16)
    return jnp.concatenate([high, middle, low], axis=0)


def terms_of(sums, x, p, u):
    mean_gain = 0.5 * press_gain
    out = [
        bond_stiff * (sums[8 + k] - u[k] * sums[11])
        - mean_gain * (p * (sums[k] - x[k] * sums[7]) + (sums[4 + k] - x[k] * sums[3]))
        for k in range(3)
    ]
    out.append(leak_gain * (sums[3] - p * sums[7]))
    return out


def block_rows(ref, first, count, stride):
    return ref[pl.ds(first, count, stride=stride), :]


def turn(blocks, turned_ref):
    for g in range(turned_ref.shape[0]):
        group = jnp.concatenate([blocks(16 * g + n) for n in range(16)], axis=0)
        turned_ref[g] = 0.5 * jnp.transpose(group)


def bond_weights(others, owned, words, bits):
    apart = [others[k] - 0.5 * owned[k : k + 1] for k in range(3)]
    size = apart[0] * apart[0] + 1.0 + (apart[1] * apart[1] + apart[2] * apart[2])
    weight = pltpu.reciprocal(size, approx=True)
    intact = (words & bits) != 0
    high = weight.astype(bf16)
    low = (weight - high.astype(f32)).astype(bf16)
    none = jnp.zeros((128, 128), bf16)
    intact_high = jnp.where(intact, high, none)
    intact_low = jnp.where(intact, low, none)
    return intact_high, high, intact_low, low


def split_sums(product):
    product = product[0:16] + product[16:32] + product[32:48]
    intact, every = product[:, :128], product[:, 128:]
    return jnp.concatenate([every[0:8] - intact[0:8], intact[8:16]], axis=0)


def tile_sums(weights, owned_feature, other_feature):
    intact_high, high, intact_low, low = weights
    by_other = jnp.concatenate(
        [
            jnp.concatenate([intact_high, high], axis=1),
            jnp.concatenate([intact_low, low], axis=1),
        ],
        axis=0,
    )
    on_owned = jnp.dot(
        jnp.concatenate([other_feature, other_feature], axis=1),
        by_other,
        preferred_element_type=f32,
    )
    by_owned = jnp.concatenate(
        [
            jnp.concatenate([intact_high, intact_low], axis=1),
            jnp.concatenate([high, low], axis=1),
        ],
        axis=0,
    )
    on_other = lax.dot_general(
        jnp.concatenate([owned_feature, owned_feature], axis=1),
        by_owned,
        (((1,), (1,)), ((), ())),
        preferred_element_type=f32,
    )
    return split_sums(on_owned), split_sums(on_other)


def tile_loop(
    slots, touch, per_step, owned_of, other_of, other_block, words_of, turned_ref, points_ref,
    feature_ref, sums_ref, weights_ref, other_feature_ref, store_other,
):
    bits = jnp.left_shift(1, lax.broadcasted_iota(jnp.int32, (16, 8, 128), 1)).reshape(128, 128)
    steps = slots // per_step

    def weigh(step, half):
        for n in range(per_step):
            slot = step * per_step + n
            other = other_of(slot)
            if other_block is not None:
                other_feature_ref[half, n] = features(other_block(slot))
            turned = turned_ref[other // 16]
            lane = 8 * lax.rem(other, 16)
            others = [
                jnp.take_along_axis(turned, jnp.full((128, 128), lane + k, jnp.int32), axis=1)
                for k in range(3)
            ]
            for e in range(touch):
                owned = owned_of(slot, e)
                a, b, c, d = bond_weights(others, points_ref[owned], words_of(slot, e), bits)
                at = n * touch + e
                weights_ref[half, at, 0:128, 0:128] = a
                weights_ref[half, at, 0:128, 128:256] = b
                weights_ref[half, at, 128:256, 0:128] = c
                weights_ref[half, at, 128:256, 128:256] = d

    def add_up(step, half):
        for n in range(per_step):
            slot = step * per_step + n
            if other_block is not None:
                feature = other_feature_ref[half, n]
            else:
                feature = feature_ref[other_of(slot)]
            on_other = None
            for e in range(touch):
                owned = owned_of(slot, e)
                kept = weights_ref[half, n * touch + e]
                parts = (kept[:128, :128], kept[:128, 128:], kept[128:, :128], kept[128:, 128:])
                on_owned, more = tile_sums(parts, feature_ref[owned], feature)
                sums_ref[owned] += on_owned
                on_other = more if on_other is None else on_other + more
            store_other(slot, on_other)

    weigh(0, 0)

    def body(k, carry):
        for n in range(4):
            weigh(4 * k + n + 1, (n + 1) % 4)
            add_up(4 * k + n, n)
        return carry

    lax.fori_loop(0, steps // 4 - 1, body, 0)
    for n in range(4):
        if n < 3:
            weigh(steps - 3 + n, n + 1)
        add_up(steps - 4 + n, n)


def block_terms(sums_ref, first, blocks_ref, count, put):
    sums = sums_ref.reshape(sums_ref.shape[0] * 16, 128)
    rows = blocks_ref.reshape(blocks_ref.shape[0] * 8, 128)
    for n in range(0, count, 16):
        own = [block_rows(rows, 8 * (first + n) + r, 16, 8) for r in range(7)]
        terms = terms_of(
            [block_rows(sums, 16 * (first + n) + r, 16, 16) for r in range(12)],
            own[0:3],
            own[3],
            own[4:7],
        )
        for k, row in enumerate(terms):
            put(k, n, row)


def fetch(copies):
    for copy in copies:
        copy.start()
    for copy in copies:
        copy.wait()


def pack_kernel(
    sends_any, moves_any, positions_any, fields_any, out_any, points_any,
    sends_ref, moves_ref, positions_ref, fields_ref, out_ref, points_ref, sems,
):
    pairs = (
        (positions_any, positions_ref),
        (fields_any, fields_ref),
        (sends_any, sends_ref),
        (moves_any, moves_ref),
    )
    fetch([pltpu.make_async_copy(a, b, sems.at[n]) for n, (a, b) in enumerate(pairs)])
    count = positions_ref.shape[1]
    flat = points_ref.reshape(count * 8, 128)
    for k in range(3):
        flat[pl.ds(k, count, stride=8), :] = positions_ref[k]
        flat[pl.ds(4 + k, count, stride=8), :] = block_rows(fields_ref, k, count, 4)
    flat[pl.ds(3, count, stride=8), :] = block_rows(fields_ref, 3, count, 4)
    flat[pl.ds(7, count, stride=8), :] = jnp.zeros((count, 128), f32)
    away = [pltpu.make_async_copy(points_ref, points_any, sems.at[4])]
    away[0].start()
    last = lax.broadcasted_iota(jnp.int32, (8, 128), 0) == 7

    def one_peer(peer, carry):
        move = moves_ref[0, 0, peer]
        moved = points_ref[jnp.maximum(move, 0)]
        moved = jnp.where(move >= 0, moved, jnp.zeros_like(moved))
        for o in range(3):
            block = points_ref[sends_ref[o, 0, peer]]
            out_ref[peer, 8 * o : 8 * o + 8] = jnp.where(last, moved[o : o + 1], block)
        return carry

    peers = out_ref.shape[0]
    for n in range(4):
        low, high = n * peers // 4, (n + 1) * peers // 4
        lax.fori_loop(low, high, one_peer, 0, unroll=True)
        away.append(pltpu.make_async_copy(out_ref.at[low:high], out_any.at[low:high], sems.at[5 + n]))
        away[-1].start()
    for copy in away:
        copy.wait()


def local_kernel(
    pairs_ref, points_ref, mask_ref, totals_ref, feature_ref, sums_ref, turned_ref, weights_ref
):
    count = points_ref.shape[0]
    tiles = mask_ref.shape[0]
    sums_ref[...] = jnp.zeros_like(sums_ref)
    turn(lambda n: points_ref[n], turned_ref)

    def one_block(block, carry):
        feature_ref[block] = features(points_ref[block])
        return carry

    lax.fori_loop(0, count, one_block, 0, unroll=8)

    def words_of(slot, e):
        return jnp.broadcast_to(mask_ref[slot][:, None, :], (16, 8, 128)).reshape(128, 128)

    def store_other(slot, on_other):
        sums_ref[pairs_ref[1, slot]] += on_other

    tile_loop(
        tiles, 1, 4, lambda slot, e: pairs_ref[0, slot], lambda slot: pairs_ref[1, slot], None,
        words_of, turned_ref, points_ref, feature_ref, sums_ref, weights_ref, None, store_other,
    )

    def put(k, n, row):
        totals_ref[k, n : n + 16] = row

    block_terms(sums_ref, 0, points_ref, count, put)


def remote_kernel(parts, adds, earlier, local_ref, points_ref, feature_ref, mask_ref, *rest):
    sources, rest = rest[: len(parts)], rest[len(parts) :]
    add_refs, rest = rest[:adds], rest[adds:]
    earlier_refs, rest = rest[:earlier], rest[earlier:]
    totals_ref, rest = rest[0], rest[1:]
    back, rest = rest[: len(parts)], rest[len(parts) :]
    sums_ref, turned_ref, weights_ref, other_feature_ref, other_sums, blocks_ref = rest
    count = points_ref.shape[0]
    per_part = parts[0][3]
    slots = per_part * len(parts)
    starts = [group * first_of_group + first for group, _, first, _, first_of_group in parts]
    for n, (_, row, first, _, _) in enumerate(parts):
        for m in range(per_part):
            blocks_ref[n * per_part + m] = sources[n][first + m, row : row + 8]
    turn(lambda n: blocks_ref[n], turned_ref)
    sums_ref[...] = jnp.zeros_like(sums_ref)
    gap = starts[-1] - starts[0] - per_part

    def entry(slot):
        return slot + starts[0] + gap * (slot // per_part)

    def owned_of(slot, e):
        return local_ref[e, entry(slot)]

    def words_of(slot, e):
        tile = 2 * entry(slot) + e
        return jnp.broadcast_to(mask_ref[tile][:, None, :], (16, 8, 128)).reshape(128, 128)

    def store_other(slot, on_other):
        other_sums[slot] = on_other

    tile_loop(
        slots, 2, 2, owned_of, lambda slot: slot, lambda slot: blocks_ref[slot], words_of, turned_ref,
        points_ref, feature_ref, sums_ref, weights_ref, other_feature_ref, store_other,
    )
    for part in range(len(parts)):
        before = back[part].shape[0] - per_part
        if before:
            back[part][0:before] = earlier_refs[part][...]
        rows = back[part].reshape(back[part].shape[0] * 4, 128)

        def put_back(k, n, row):
            rows[pl.ds(4 * (before + n) + k, 16, stride=4), :] = row

        block_terms(other_sums, part * per_part, blocks_ref, per_part, put_back)

    def put(k, n, row):
        for add in add_refs:
            row = row + add[k, n : n + 16]
        totals_ref[k, n : n + 16] = row

    block_terms(sums_ref, 0, points_ref, count, put)


def update_kernel(
    sends_ref, moves_ref, totals_ref, returned_ref, fields_ref, velocity_ref, storage_ref,
    new_fields_ref, new_velocity_ref, moving_ref, down_ref, here_ref, up_ref, rows_ref,
):
    count = storage_ref.shape[0]
    peers = returned_ref.shape[0]
    sums_refs = (down_ref, here_ref, up_ref)
    for sums_ref in sums_refs:
        sums_ref[...] = jnp.zeros_like(sums_ref)

    def one_peer(peer, carry):
        for o, sums_ref in enumerate(sums_refs):
            sums_ref[sends_ref[o, 0, peer]] += returned_ref[peer, o]
        return carry

    lax.fori_loop(0, peers, one_peer, 0, unroll=True)
    flats = [sums_ref.reshape(count * 4, 128) for sums_ref in sums_refs]

    def total(k):
        down, here, up = (block_rows(flat, k, count, 4) for flat in flats)
        return totals_ref[k] + (down + here + up)

    rows = rows_ref.reshape(count * 8, 128)
    for k in range(3):
        speed = velocity_ref[k] + time_step * total(k)
        moved = block_rows(fields_ref, k, count, 4) + time_step * speed
        new_velocity_ref[k] = speed
        new_fields_ref[pl.ds(k, count, stride=4), :] = moved
        rows[pl.ds(k, count, stride=8), :] = moved
        rows[pl.ds(4 + k, count, stride=8), :] = speed
    stored = storage_ref[...]
    pressure = (
        block_rows(fields_ref, 3, count, 4)
        + time_step * total(3) / stored
    )
    new_fields_ref[pl.ds(3, count, stride=4), :] = pressure
    rows[pl.ds(3, count, stride=8), :] = pressure
    rows[pl.ds(7, count, stride=8), :] = stored

    def one_move(peer, carry):
        move = moves_ref[0, 0, peer]
        block = rows_ref[jnp.maximum(move, 0)]
        moving_ref[peer] = jnp.where(move >= 0, block, jnp.zeros_like(block))
        return carry

    lax.fori_loop(0, peers, one_move, 0, unroll=True)


def arrive_kernel(late_ref, early_ref, out_ref):
    peers = late_ref.shape[0]
    late = late_ref.reshape(peers * 8, 128)
    early = early_ref.reshape(peers * 24, 128)
    for k in range(7):
        out_ref[k] = block_rows(late, k, peers, 8)
    for k in range(3):
        out_ref[7 + k] = block_rows(early, 8 * k + 7, peers, 24)
    out_ref[10] = block_rows(late, 7, peers, 8)


def in_vmem():
    return pl.BlockSpec(memory_space=pltpu.VMEM)


def in_smem():
    return pl.BlockSpec(memory_space=pltpu.SMEM)


def params():
    return pltpu.CompilerParams(vmem_limit_bytes=vmem_bytes)


def cost(flops):
    return pl.CostEstimate(flops=flops, bytes_accessed=2 * 1024 * 1024, transcendentals=0)


def shape(*dims, dtype=f32):
    return jax.ShapeDtypeStruct(dims, dtype)


def anywhere():
    return pl.BlockSpec(memory_space=pl.ANY)


def remote_tiles(parts, local, points, feature, mask, sources, adds=(), earlier=()):
    count = points.shape[0]
    per_part = parts[0][3]
    slots = per_part * len(parts)
    before = earlier[0].shape[0] if earlier else 0
    return pl.pallas_call(
        functools.partial(remote_kernel, parts, len(adds), len(earlier)),
        out_shape=[shape(4, count, 128)] + [shape(before + per_part, 4, 128)] * len(parts),
        in_specs=[in_smem()] + [in_vmem()] * (3 + len(sources) + len(adds) + len(earlier)),
        out_specs=[in_vmem()] * (1 + len(parts)),
        scratch_shapes=[
            pltpu.VMEM((count, 16, 128), f32),
            pltpu.VMEM((slots // 16, 128, 128), f32),
            pltpu.VMEM((4, 4, 256, 256), bf16),
            pltpu.VMEM((4, 2, 48, 128), bf16),
            pltpu.VMEM((slots, 16, 128), f32),
            pltpu.VMEM((slots, 8, 128), f32),
        ],
        compiler_params=params(),
        cost_estimate=cost(slots * 10**8),
        name="remote_tiles",
    )(local, points, feature, mask, *sources, *adds, *earlier)


def local_tiles(pairs, points, mask):
    count = points.shape[0]
    return pl.pallas_call(
        local_kernel,
        out_shape=[shape(4, count, 128), shape(count, 48, 128, dtype=bf16)],
        in_specs=[in_smem(), in_vmem(), in_vmem()],
        out_specs=[in_vmem()] * 2,
        scratch_shapes=[
            pltpu.VMEM((count, 16, 128), f32),
            pltpu.VMEM((count // 16, 128, 128), f32),
            pltpu.VMEM((4, 4, 256, 256), bf16),
        ],
        compiler_params=params(),
        cost_estimate=cost(4 * 10**9),
        name="local_tiles",
    )(pairs, points, mask)


def per_device(
    positions,
    fields,
    storage,
    velocity,
    send_list,
    remote_local,
    remote_mask,
    local_pairs,
    local_mask,
    migrate_list,
):
    count = positions.shape[0]
    peers = send_list.shape[2]
    sends = send_list[0].transpose(0, 2, 1)
    moves = migrate_list.transpose(0, 2, 1)
    rows_first = positions.transpose(1, 0, 2)
    flat_fields = fields.reshape(count * 4, 128)
    outgoing, points = pl.pallas_call(
        pack_kernel,
        out_shape=[shape(peers, 24, 128), shape(count, 8, 128)],
        in_specs=[anywhere()] * 4,
        out_specs=[anywhere()] * 2,
        scratch_shapes=[
            pltpu.SMEM(sends.shape, jnp.int32),
            pltpu.SMEM(moves.shape, jnp.int32),
            pltpu.VMEM(rows_first.shape, f32),
            pltpu.VMEM(flat_fields.shape, f32),
            pltpu.VMEM((peers, 24, 128), f32),
            pltpu.VMEM((count, 8, 128), f32),
            pltpu.SemaphoreType.DMA((9,)),
        ],
        compiler_params=pltpu.CompilerParams(vmem_limit_bytes=60 * 1024 * 1024),
        name="pack",
    )(sends, moves, rows_first, flat_fields)
    spread = lax.all_to_all(outgoing, "bulk", split_axis=0, concat_axis=0, tiled=True)
    local_totals, feature = local_tiles(local_pairs[0].transpose(1, 0), points, local_mask[0])
    spread, feature = lax.optimization_barrier((spread, feature))
    local = remote_local[0].transpose(1, 0)
    mask = remote_mask[0].reshape(-1, remote_mask.shape[3], remote_mask.shape[4])
    tile_args = (local, points, feature, mask)
    up = from_behind(spread[:, 16:24], "region", 1)
    down = from_behind(spread[:, 0:8], "region", -1)
    half = peers // 2
    first_totals, first_back = remote_tiles(((1, 8, 0, half, peers),), *tile_args, [spread])
    far_totals, up_back, down_back = remote_tiles(
        ((2, 0, 0, peers, peers), (0, 0, 0, peers, peers)), *tile_args, [up, down]
    )
    down_back = from_behind(down_back, "region", 1)
    up_back = from_behind(up_back, "region", -1)
    totals, here_back = remote_tiles(
        ((1, 8, half, half, peers),), *tile_args, [spread],
        [local_totals, first_totals, far_totals], [first_back],
    )
    stacked = jnp.stack([down_back, here_back, up_back], axis=1)
    returned = lax.all_to_all(stacked, "bulk", split_axis=0, concat_axis=0, tiled=True)
    new_fields, new_velocity, moving = pl.pallas_call(
        update_kernel,
        out_shape=[shape(count * 4, 128), shape(3, count, 128), shape(peers, 8, 128)],
        in_specs=[in_smem()] * 2 + [in_vmem()] * 5,
        out_specs=[in_vmem()] * 3,
        scratch_shapes=[pltpu.VMEM((count, 4, 128), f32)] * 3 + [pltpu.VMEM((count, 8, 128), f32)],
        compiler_params=params(),
        name="update",
    )(sends, moves, totals, returned, flat_fields, velocity.transpose(1, 0, 2), storage)
    late = lax.all_to_all(moving, "bulk", split_axis=0, concat_axis=0, tiled=True)
    arrived = pl.pallas_call(
        arrive_kernel,
        out_shape=shape(11, peers, 128),
        in_specs=[in_vmem()] * 2,
        out_specs=in_vmem(),
        compiler_params=params(),
        name="arrive",
    )(late, spread)
    return (
        new_fields.reshape(count, 4, 128),
        new_velocity.transpose(1, 0, 2),
        arrived.transpose(1, 0, 2),
    )


def solution(mesh):
    spec = lambda rank: P(("region", "bulk"), *([None] * (rank - 1)))
    return jax.shard_map(
        per_device,
        mesh=mesh,
        in_specs=tuple(spec(rank) for rank in (3, 3, 2, 3, 4, 3, 5, 3, 4, 3)),
        out_specs=(spec(3), spec(3), spec(3)),
        check_vma=False,
    )
```
